32 devices in a mesh: gx: 8 (over z, y), gy: 4 (over x, core).
Axes of the slice: x: 2, y: 2, z: 4, core: 2. Of those that a mesh axis runs over, the one named last changes fastest.
Arguments:
- initial_state: float32 [32, 2, 256, 1024], P(None, None, 'gy', 'gx'), may hold values from -34 to 34
- velocity: float32 [3, 2, 256, 1024], P(None, None, 'gy', 'gx'), may hold values from -0.3 to 0.3
- diffusivity: float32 [32], replicated, may hold values from 0.02 to 0.15
- reaction_rate: float32 [32], replicated, may hold values from 0.05 to 0.5
- start_basis: bfloat16 [1024, 128], replicated, may hold values from -0.1875 to 0.1875
Outputs:
- evolved: float32 [32, 2, 256, 1024], P(None, None, 'gy', 'gx')
- factor: bfloat16 [1024, 128], P(('gx', 'gy'))
- subspace_core: float32 [32, 2, 256, 128], P('gx', None, 'gy')
The draws below stay inside these ranges and needn't reach their ends.
All inputs are finite; a program needn't handle non-finite values.
Results may differ from the reference program's by a relative error of at most 0.012.
Values may be sent and summed in bfloat16 or wider, within the bound.
No kernel may reach another device: no remote copies, remote signals or barrier semaphores. Data moves between devices by JAX's collectives and lax.ppermute only.
A program may use at most 64 MiB of HBM per device.

```python
import math
import jax
import jax.numpy as jnp
from jax import lax

SPECIES = 32
RANK = 128
SECTIONS = 4
NS_STEPS = 5
NZ = 2
NX = 1024
NY = 256


def draw_initial_state(key, part):
    subkeys = jax.random.split(jax.random.fold_in(key, 11), 3)
    values = jax.random.truncated_normal(subkeys[0], -4.0, 4.0, (SPECIES, NZ, NY, NX), jnp.float32)
    row_scale = jnp.exp(math.log(3.0) * jnp.arange(NX, dtype=jnp.float32) / NX)
    species = jnp.exp(jax.random.uniform(subkeys[2], (SPECIES,), jnp.float32, math.log(0.5), math.log(2.0)))
    return values * species[:, None, None, None] * row_scale


def steps_of(key, dims, pieces, low, largest):
    level = 1.0
    for axis_at, blocks in pieces:
        draws = jax.random.uniform(jax.random.fold_in(jax.random.fold_in(key, 6), axis_at), (blocks,), jnp.float32, low / len(pieces), largest / len(pieces))
        level = level * jnp.repeat(jnp.exp(draws), dims[axis_at] // blocks).reshape((-1,) + (1,) * (len(dims) - 1 - axis_at))
    return level


def bell_draw(stream_key, shape, spread, limit, held_as=jnp.bfloat16):
    entries = spread * jax.random.normal(stream_key, shape, jnp.float32)
    return jnp.clip(entries, min=-limit, max=limit).astype(held_as)


def setup_inputs(seed: int = 0) -> dict:
    key_of = jax.random.split(jax.random.key(seed), 6)
    return {
        "initial_state": draw_initial_state(jax.random.fold_in(key_of[5], 71), 0),
        "velocity": jnp.clip(jax.random.uniform(key_of[1], (3, NZ, NY, NX), jnp.float32, -0.3, 0.3) * steps_of(key_of[1], (3, NZ, NY, NX), ((2, 4), (3, 8)), -0.4, 0.0), -0.3, 0.3),
        "diffusivity": jnp.clip(jnp.exp(jax.random.uniform(key_of[2], (SPECIES,), jnp.float32, math.log(0.02), math.log(0.15))), 0.02, 0.15),
        "reaction_rate": jnp.clip(jnp.exp(jax.random.uniform(key_of[3], (SPECIES,), jnp.float32, math.log(0.05), math.log(0.5))), 0.05, 0.5),
        "start_basis": bell_draw(key_of[4], (NX, RANK), NX ** -0.5, 0.1875),
    }


def advance(field_now, velocity, diffusivity, reaction_rate):
    walled = jnp.pad(field_now, ((1, 1), (0, 0), (0, 0)))
    upper_side = walled[2:]
    lower_side = walled[:-2]
    north_side = jnp.roll(field_now, -1, axis=1)
    south_side = jnp.roll(field_now, 1, axis=1)
    east_side = jnp.roll(field_now, -1, axis=2)
    west_side = jnp.roll(field_now, 1, axis=2)
    laplacian = east_side + west_side + north_side + south_side + upper_side + lower_side - 6.0 * field_now
    transport = velocity[0] * (east_side - west_side) + velocity[1] * (north_side - south_side) + velocity[2] * (upper_side - lower_side)
    decay = reaction_rate * field_now * field_now * field_now / (1.0 + field_now * field_now)
    return field_now + diffusivity * laplacian - 0.5 * transport - decay

def reference(initial_state, velocity, diffusivity, reaction_rate, start_basis):

    def evolve(inputs):
        field_now, kappa_one, rate_one = inputs
        for section_index in range(SECTIONS):
            field_now = advance(field_now, velocity, kappa_one, rate_one)
        return field_now
    evolved = lax.map(evolve, (initial_state, diffusivity, reaction_rate))
    columns = evolved.astype(jnp.bfloat16).reshape(SPECIES * NZ * NY, NX)
    project = jnp.dot(columns, start_basis, preferred_element_type=jnp.float32).astype(jnp.bfloat16)
    images = lax.dot_general(columns, project, (((0,), (0,)), ((), ())), preferred_element_type=jnp.float32)
    highest = lax.Precision.HIGHEST
    identity = jnp.eye(RANK, dtype=jnp.float32)
    gram_matrix = jnp.dot(images.T, images, precision=highest)
    scaling = jnp.sqrt(NX / (jnp.trace(gram_matrix) + 1e-06))
    factor = images * scaling
    for section_index in range(NS_STEPS):
        gram_matrix = jnp.dot(factor.T, factor, precision=highest) / NX
        factor = jnp.dot(factor, 1.5 * identity - 0.5 * gram_matrix, precision=highest)
    factor = factor.astype(jnp.bfloat16)
    subspace_core = jnp.dot(columns, factor, preferred_element_type=jnp.float32) / math.sqrt(NX)
    return (evolved, factor, subspace_core.reshape(SPECIES, NZ, NY, RANK))
```

```python
import functools
import math

import jax
import jax.numpy as jnp
from jax import lax
from jax.experimental import pallas as pl
from jax.experimental.pallas import tpu as pltpu
from jax.sharding import PartitionSpec as P

SECTIONS = 4
NS_STEPS = 5
HIGHEST = lax.Precision.HIGHEST
VMEM_BYTES = 48 * 1024 * 1024
BOTH = ("gx", "gy")


def with_halo(x, sides, width):
    for axis, dim in sides:
        count, length = (lax.axis_size(axis), x.shape[dim])
        up = [(i, (i + 1) % count) for i in range(count)]
        down = [(j, i) for i, j in up]
        last = lax.slice_in_dim(x, length - width, length, axis=dim)
        initial = lax.slice_in_dim(x, 0, width, axis=dim)
        before = lax.ppermute(last, axis, up)
        after = lax.ppermute(initial, axis, down)
        x = jnp.concatenate([before, x, after], axis=dim)
    return x


def advance(padded, velocity, diffusivity, reaction_rate):
    centre = padded[:, :, 1:-1, 1:-1]
    east_side = padded[:, :, 1:-1, 2:]
    west_side = padded[:, :, 1:-1, :-2]
    north_side = padded[:, :, 2:, 1:-1]
    south_side = padded[:, :, :-2, 1:-1]
    walled = jnp.pad(centre, ((0, 0), (1, 1), (0, 0), (0, 0)))
    upper_side = walled[:, 2:]
    lower_side = walled[:, :-2]
    laplacian = (
        east_side + west_side + north_side + south_side + upper_side + lower_side - 6.0 * centre
    )
    transport = (
        velocity[0] * (east_side - west_side)
        + velocity[1] * (north_side - south_side)
        + velocity[2] * (upper_side - lower_side)
    )
    decay = reaction_rate[:, None, None, None] * centre * centre * centre / (1.0 + centre * centre)
    return centre + diffusivity[:, None, None, None] * laplacian - 0.5 * transport - decay


def image_kernel(columns_ref, basis_ref, image_ref):
    pieces, rows, width = columns_ref.shape
    project = jnp.zeros((rows, basis_ref.shape[1]), jnp.float32)
    for piece in range(pieces):
        project += jnp.dot(
            columns_ref[piece],
            basis_ref[pl.ds(piece * width, width), :],
            preferred_element_type=jnp.float32,
        )
    project = project.astype(jnp.bfloat16)
    for piece in range(pieces):
        image_ref[pl.ds(piece * width, width), :] = lax.dot_general(
            columns_ref[piece],
            project,
            (((0,), (0,)), ((), ())),
            preferred_element_type=jnp.float32,
        ).astype(image_ref.dtype)


def factor_kernel(owner_ref, image_ref, columns_ref, own_ref, core_ref, factor_ref):
    pieces, rows, width = columns_ref.shape
    rows_all, rank = image_ref.shape
    rows_each = own_ref.shape[0]
    image = image_ref[...]
    row = lax.broadcasted_iota(jnp.int32, (rank, rank), 0)
    column = lax.broadcasted_iota(jnp.int32, (rank, rank), 1)
    identity = (row == column).astype(jnp.float32)
    gram = lax.dot_general(
        image,
        image,
        (((0,), (0,)), ((), ())),
        precision=HIGHEST,
        preferred_element_type=jnp.float32,
    )
    trace = jnp.sum(gram * identity)
    gram = gram / (trace + 1e-06)
    product = None
    for step in range(NS_STEPS):
        update = 1.5 * identity - 0.5 * gram
        if step < NS_STEPS - 1:
            gram = jnp.dot(gram, update, precision=HIGHEST, preferred_element_type=jnp.float32)
            gram = jnp.dot(update, gram, precision=HIGHEST, preferred_element_type=jnp.float32)
        if product is None:
            product = update
        else:
            product = jnp.dot(
                product, update, precision=HIGHEST, preferred_element_type=jnp.float32
            )
    scaling = jnp.sqrt(rows_all / (trace + 1e-06))
    factor = jnp.dot(
        image * scaling, product, precision=HIGHEST, preferred_element_type=jnp.float32
    )
    factor_ref[...] = factor.astype(jnp.bfloat16)
    start = pl.multiple_of(owner_ref[0] * rows_each, rows_each)
    own_ref[...] = factor_ref[pl.ds(start, rows_each), :]
    core = jnp.zeros((rows, rank), jnp.float32)
    for piece in range(pieces):
        core += jnp.dot(
            columns_ref[piece],
            factor_ref[pl.ds(piece * width, width), :],
            preferred_element_type=jnp.float32,
        )
    core_ref[...] = core / math.sqrt(rows_all)


def vmem(count):
    return [pl.BlockSpec(memory_space=pltpu.VMEM)] * count


def subspace(columns, start_basis):
    pieces, rows, width = columns.shape
    rows_all, rank = start_basis.shape
    owners = lax.axis_size(BOTH)
    rows_each = rows_all // owners
    params = pltpu.CompilerParams(vmem_limit_bytes=VMEM_BYTES)
    partial = pl.pallas_call(
        image_kernel,
        out_shape=jax.ShapeDtypeStruct((rows_all, rank), jnp.float32),
        in_specs=vmem(2),
        out_specs=vmem(1)[0],
        compiler_params=params,
    )(columns, start_basis)
    shares = lax.all_to_all(
        partial.reshape(owners, rows_each, rank), BOTH, split_axis=0, concat_axis=0, tiled=True
    )
    own_image = jnp.sum(shares, axis=0)
    image = lax.all_to_all(
        jnp.broadcast_to(own_image[None], (owners, rows_each, rank)),
        BOTH,
        split_axis=0,
        concat_axis=0,
        tiled=True,
    ).reshape(rows_all, rank)
    owner = lax.axis_index(BOTH).astype(jnp.int32).reshape(1)
    return pl.pallas_call(
        factor_kernel,
        out_shape=(
            jax.ShapeDtypeStruct((rows_each, rank), jnp.bfloat16),
            jax.ShapeDtypeStruct((rows, rank), jnp.float32),
        ),
        in_specs=[pl.BlockSpec(memory_space=pltpu.SMEM)] + vmem(2),
        out_specs=tuple(vmem(2)),
        scratch_shapes=[pltpu.VMEM((rows_all, rank), jnp.bfloat16)],
        compiler_params=params,
    )(owner, image, columns)


def shards(initial_state, velocity, diffusivity, reaction_rate, start_basis):
    field_now = initial_state
    for section_index in range(SECTIONS):
        padded = with_halo(field_now, (("gx", 3), ("gy", 2)), 1)
        field_now = advance(padded, velocity, diffusivity, reaction_rate)
    species, heights, length, width = field_now.shape
    pieces = lax.axis_size("gx")
    each = species // pieces
    columns = lax.all_to_all(
        field_now.astype(jnp.bfloat16), "gx", split_axis=0, concat_axis=0, tiled=True
    ).reshape(pieces, each * heights * length, width)
    own_rows, core = subspace(columns, start_basis)
    return (field_now, own_rows, core.reshape(each, heights, length, start_basis.shape[1]))


def solution(mesh):
    in_specs = (P(None, None, "gy", "gx"), P(None, None, "gy", "gx"), P(), P(), P())
    out_specs = (P(None, None, "gy", "gx"), P(("gx", "gy"), None), P("gx", None, "gy", None))
    return jax.shard_map(shards, mesh=mesh, in_specs=in_specs, out_specs=out_specs, check_vma=False)
```

```python
import math

import jax
import jax.numpy as jnp
from jax import lax
from jax.experimental import pallas as pl
from jax.experimental.pallas import tpu as pltpu
from jax.sharding import PartitionSpec as P

SECTIONS = 4
NS_STEPS = 5
HIGHEST = lax.Precision.HIGHEST
VMEM_BYTES = 48 * 1024 * 1024
BOTH = ("gx", "gy")
LANES = 128
WIDTH = SECTIONS
WINDOW = 2 * WIDTH


def near_pairs(count):
    return [(i, i ^ 1) for i in range(count)]


def far_pairs(count):
    return [(i, (i + 1) % count if i % 2 else (i - 1) % count) for i in range(count)]


def swap_near(x, axis):
    return lax.ppermute(x, axis, near_pairs(lax.axis_size(axis)))


def swap_far(x, axis):
    return lax.ppermute(x, axis, far_pairs(lax.axis_size(axis)))


def iota(shape, dim):
    return lax.broadcasted_iota(jnp.int32, shape, dim)


def place_edges(tile, slot, packed):
    width = tile.shape[1]
    lane = iota((tile.shape[0], LANES), 1)
    both = tile
    if width > LANES:
        both = jnp.where(lane < WIDTH, tile[:, :LANES], tile[:, width - LANES :])
    rolled = pltpu.roll(both, WIDTH + WINDOW * slot, 1) if WIDTH + WINDOW * slot < LANES else (
        pltpu.roll(both, WIDTH + WINDOW * slot - LANES, 1)
    )
    return jnp.where(lane // WINDOW == slot, rolled, packed)


def pack_kernel(parity_ref, state_ref, velocity_ref, near_ref, far_ref, edges_ref):
    species, heights, length, width = state_ref.shape
    components = velocity_ref.shape[0]
    even = parity_ref[0] == 0
    sub = iota((8, width), 0)

    def edge_rows(ref, at):
        first = [ref[at, z, pl.ds(0, 8), :] for z in range(2)]
        last = [ref[at, z, pl.ds(length - 8, 8), :] for z in range(2)]
        first = jnp.where(sub < WIDTH, first[0], pltpu.roll(first[1], WIDTH, 0))
        last = jnp.where(sub < WIDTH, pltpu.roll(last[0], WIDTH, 0), last[1])
        return jnp.where(even, last, first), jnp.where(even, first, last)

    def put(pair, one, two):
        near_ref[pair] = jnp.concatenate([one[0], two[0]], axis=0).astype(jnp.bfloat16)
        far_ref[pair] = jnp.concatenate([one[1], two[1]], axis=0).astype(jnp.bfloat16)

    def pair_body(pair, carry):
        put(pair, edge_rows(state_ref, 2 * pair), edge_rows(state_ref, 2 * pair + 1))
        return carry

    lax.fori_loop(0, species // 2, pair_body, 0, unroll=2)
    flows = [edge_rows(velocity_ref, at) for at in range(components)]
    put(species // 2, flows[0], flows[1])
    put(species // 2 + 1, flows[2], flows[2])

    per_group = LANES // WINDOW

    def rows_body(at, carry):
        start = pl.multiple_of(at * 16, 16)
        for z in range(heights):
            target = pl.ds(pl.multiple_of(z * length + start, 16), 16)
            for group in range(species // per_group):
                packed = jnp.zeros((16, LANES), jnp.float32)
                for slot in range(per_group):
                    tile = state_ref[group * per_group + slot, z, pl.ds(start, 16), :]
                    packed = place_edges(tile, slot, packed)
                edges_ref[group, target, :] = packed.astype(jnp.bfloat16)
            packed = jnp.zeros((16, LANES), jnp.float32)
            for slot in range(components):
                packed = place_edges(velocity_ref[slot, z, pl.ds(start, 16), :], slot, packed)
            edges_ref[species // per_group, target, :] = packed.astype(jnp.bfloat16)
        return carry

    lax.fori_loop(0, length // 16, rows_body, 0)


def halo_kernel(parity_ref, near_ref, far_ref, velocity_ref, old_ref, rows_ref, half_ref, edges_ref):
    species, _, width = rows_ref.shape
    components, heights, length, _ = velocity_ref.shape
    even = parity_ref[0] == 0
    sub = iota((8, width), 0)
    per_group = LANES // WINDOW

    def tile_of(at):
        near = near_ref[at // 2].astype(jnp.float32)[8 * (at % 2) : 8 * (at % 2) + 8]
        far = far_ref[at // 2].astype(jnp.float32)[8 * (at % 2) : 8 * (at % 2) + 8]
        after = jnp.where(even, near, far)
        before = jnp.where(even, far, near)
        one = jnp.where(sub < WIDTH, after, pltpu.roll(before, WIDTH, 0))
        two = jnp.where(sub < WIDTH, pltpu.roll(after, WIDTH, 0), before)
        return jnp.concatenate([one, two], axis=0)

    for group in range(species // per_group):
        packed = jnp.zeros((16, LANES), jnp.float32)
        for slot in range(per_group):
            tile = tile_of(group * per_group + slot)
            rows_ref[group * per_group + slot] = tile
            packed = place_edges(tile, slot, packed)
        edges_ref[group] = packed.astype(jnp.bfloat16)
    packed = jnp.zeros((16, LANES), jnp.float32)
    for slot in range(components):
        tile = tile_of(species + slot)
        packed = place_edges(tile, slot, packed)
        for z in range(heights):
            factor = -0.5 if slot == 2 and z == 1 else 0.5
            half_ref[slot, z, pl.ds(0, length), :] = factor * velocity_ref[slot, z]
            half_ref[slot, z, pl.ds(length, 8), :] = factor * tile[8 * z : 8 * z + 8]
    edges_ref[species // per_group] = packed.astype(jnp.bfloat16)


def advance(here, other, east, west, flow, diffusion, rate):
    north = pltpu.roll(here, here.shape[0] - 1, 0)
    south = pltpu.roll(here, 1, 0)
    square = 1.0 + here * here
    inverse = pl.reciprocal(square, approx=True)
    inverse = inverse * (2.0 - square * inverse)
    centre = here * ((1.0 - 6.0 * diffusion - rate) + rate * inverse)
    spread = diffusion * ((east + west) + (north + south))
    moved = flow[0] * (east - west) + flow[1] * (north - south)
    return (centre + other * (diffusion - flow[2])) + (spread - moved)


def window_kernel(parity_ref, own_ref, near_ref, far_ref, spread_ref, rate_ref, border_ref):
    sections, groups, heights, rows, _ = border_ref.shape
    length = rows - 8
    even = parity_ref[0] == 0
    lane = iota((rows, LANES), 1)
    low = lane % WINDOW < WIDTH

    def rows_of(ref, group, z):
        whole = ref[group].astype(jnp.float32)
        body = whole[z * length : (z + 1) * length]
        return jnp.concatenate(
            [body, whole[heights * length + 8 * z : heights * length + 8 * z + 8]], axis=0
        )

    def windows(group):
        out = []
        for z in range(heights):
            own, near, far = [rows_of(r, group, z) for r in (own_ref, near_ref, far_ref)]
            right = jnp.where(even, near, far)
            left = jnp.where(even, far, near)
            out.append((jnp.where(low, left, own), jnp.where(low, own, right)))
        return [[out[z][side] for z in range(heights)] for side in range(2)]

    def spread_lanes(packed, slot):
        part = jnp.where(lane // WINDOW == slot, packed, 0.0)
        step = WINDOW
        while step < LANES:
            part = part + pltpu.roll(part, step, 1)
            step *= 2
        return part

    flows = windows(groups)
    flow = [
        [
            [
                (-0.5 if slot == 2 and z == 1 else 0.5) * spread_lanes(flows[side][z], slot)
                for slot in range(3)
            ]
            for z in range(heights)
        ]
        for side in range(2)
    ]
    for group in range(groups):
        now = windows(group)
        diffusion = spread_ref[group]
        rate = rate_ref[group]
        for section in range(sections):
            for z in range(heights):
                border_ref[section, group, z] = jnp.where(low, now[0][z], now[1][z])
            if section == sections - 1:
                break
            now = [
                [
                    advance(
                        now[side][z],
                        now[side][1 - z],
                        pltpu.roll(now[side][z], LANES - 1, 1),
                        pltpu.roll(now[side][z], 1, 1),
                        flow[side][z],
                        diffusion,
                        rate,
                    )
                    for z in range(heights)
                ]
                for side in range(2)
            ]


def section_kernel(
    first_ref, state_ref, rows_ref, border_ref, half_ref, spread_ref, rate_ref, *rest
):
    evolved_ref, piece_ref = rest[-2:]
    _, heights, length, width = state_ref.shape
    sections = border_ref.shape[0]
    rows = length + 8
    at = first_ref[0] + pl.program_id(0)
    slot = lax.rem(at, LANES // WINDOW)
    shift = LANES - WIDTH - WINDOW * slot
    diffusion = spread_ref[at]
    rate = rate_ref[at]
    lane = iota((rows, width), 1)
    now = [
        jnp.concatenate([state_ref[0, z], rows_ref[0, pl.ds(8 * z, 8), :]], axis=0)
        for z in range(heights)
    ]
    for section in range(sections):
        later = []
        for z in range(heights):
            border = pltpu.roll(border_ref[section, 0, z], shift, 1)
            if width > LANES:
                border = jnp.concatenate([border] * (width // LANES), axis=1)
            east = pltpu.roll(jnp.where(lane == 0, border, now[z]), width - 1, 1)
            west = pltpu.roll(jnp.where(lane == width - 1, border, now[z]), 1, 1)
            flow = [half_ref[slot_at, z] for slot_at in range(3)]
            later.append(advance(now[z], now[1 - z], east, west, flow, diffusion, rate))
        now = later
    for z in range(heights):
        evolved_ref[0, z] = now[z][:length]
        piece_ref[0, pl.ds(z * length, length), :] = now[z][:length].astype(jnp.bfloat16)


def image_kernel(place_ref, basis_ref, *rest):
    columns, image_ref = rest[:-1], rest[-1]
    width = columns[0].shape[1]

    def rows_of(piece):
        return pl.ds(pl.multiple_of((place_ref[0] ^ piece) * width, width), width)

    project = jnp.zeros((columns[0].shape[0], basis_ref.shape[1]), jnp.float32)
    for piece, column in enumerate(columns):
        project += jnp.dot(
            column[...], basis_ref[rows_of(piece), :], preferred_element_type=jnp.float32
        )
    project = project.astype(jnp.bfloat16)
    for piece, column in enumerate(columns):
        image_ref[rows_of(piece), :] = lax.dot_general(
            column[...], project, (((0,), (0,)), ((), ())), preferred_element_type=jnp.float32
        ).astype(image_ref.dtype)


def factor_kernel(place_ref, image_ref, *rest):
    columns, (own_ref, core_ref, factor_ref) = rest[:-3], rest[-3:]
    rows, width = columns[0].shape
    rows_all, rank = image_ref.shape
    rows_each = own_ref.shape[0]
    image = image_ref[...]
    identity = (iota((rank, rank), 0) == iota((rank, rank), 1)).astype(jnp.float32)
    gram = lax.dot_general(
        image,
        image,
        (((0,), (0,)), ((), ())),
        precision=HIGHEST,
        preferred_element_type=jnp.float32,
    )
    trace = jnp.sum(gram * identity)
    gram = gram / (trace + 1e-06)
    product = None
    for step in range(NS_STEPS):
        update = 1.5 * identity - 0.5 * gram
        if step < NS_STEPS - 1:
            gram = jnp.dot(gram, update, precision=HIGHEST, preferred_element_type=jnp.float32)
            gram = jnp.dot(update, gram, precision=HIGHEST, preferred_element_type=jnp.float32)
        if product is None:
            product = update
        else:
            product = jnp.dot(
                product, update, precision=HIGHEST, preferred_element_type=jnp.float32
            )
    scaling = jnp.sqrt(rows_all / (trace + 1e-06))
    factor = jnp.dot(
        image * scaling, product, precision=HIGHEST, preferred_element_type=jnp.float32
    )
    factor_ref[...] = factor.astype(jnp.bfloat16)
    start = pl.multiple_of(place_ref[1] * rows_each, rows_each)
    own_ref[...] = factor_ref[pl.ds(start, rows_each), :]
    core = jnp.zeros((rows, rank), jnp.float32)
    for piece, column in enumerate(columns):
        at = pl.ds(pl.multiple_of((place_ref[0] ^ piece) * width, width), width)
        core += jnp.dot(column[...], factor_ref[at, :], preferred_element_type=jnp.float32)
    core_ref[...] = core / math.sqrt(rows_all)


def call(kernel, out_shape, inputs, **rest):
    return pl.pallas_call(
        kernel,
        out_shape=out_shape,
        compiler_params=pltpu.CompilerParams(vmem_limit_bytes=VMEM_BYTES),
        **rest,
    )(*inputs)


def vmem(count):
    return [pl.BlockSpec(memory_space=pltpu.VMEM)] * count


SCALARS = [pl.BlockSpec(memory_space=pltpu.SMEM)]


def subspace(columns, start_basis):
    rows, width = columns[0].shape
    rows_all, rank = start_basis.shape
    owners = lax.axis_size(BOTH)
    rows_each = rows_all // owners
    place = jnp.stack([lax.axis_index("gx"), lax.axis_index(BOTH)]).astype(jnp.int32)
    partial = call(
        image_kernel,
        jax.ShapeDtypeStruct((rows_all, rank), jnp.float32),
        (place, start_basis, *columns),
        in_specs=SCALARS + vmem(1 + len(columns)),
        out_specs=vmem(1)[0],
    )
    shares = lax.all_to_all(
        partial.reshape(owners, rows_each, rank), BOTH, split_axis=0, concat_axis=0, tiled=True
    )
    own_image = jnp.sum(shares, axis=0)
    image = lax.all_to_all(
        jnp.broadcast_to(own_image[None], (owners, rows_each, rank)),
        BOTH,
        split_axis=0,
        concat_axis=0,
        tiled=True,
    ).reshape(rows_all, rank)
    return call(
        factor_kernel,
        (
            jax.ShapeDtypeStruct((rows_each, rank), jnp.bfloat16),
            jax.ShapeDtypeStruct((rows, rank), jnp.float32),
        ),
        (place, image, *columns),
        in_specs=SCALARS + vmem(1 + len(columns)),
        out_specs=tuple(vmem(2)),
        scratch_shapes=[pltpu.VMEM((rows_all, rank), jnp.bfloat16)],
    )


def borders(initial_state, velocity, diffusivity, reaction_rate):
    species, heights, length, width = initial_state.shape
    groups = species * WINDOW // LANES
    parity = (lax.axis_index("gy") % 2).astype(jnp.int32).reshape(1)
    edge = jax.ShapeDtypeStruct((species // 2 + 2, 16, width), jnp.bfloat16)
    window = jax.ShapeDtypeStruct((groups + 1, heights * (length + 8), LANES), jnp.bfloat16)
    near, far, edges = call(
        pack_kernel,
        (edge, edge, window),
        (parity, initial_state, velocity),
        in_specs=SCALARS + vmem(2),
        out_specs=tuple(vmem(3)),
    )
    near = swap_near(near, "gy")
    far = swap_far(far, "gy")
    last = heights * length // 16
    halo_rows, half, edges = call(
        halo_kernel,
        (
            jax.ShapeDtypeStruct((species, 16, width), jnp.float32),
            jax.ShapeDtypeStruct((3, heights, length + 8, width), jnp.float32),
            window,
        ),
        (parity, near, far, velocity, edges),
        grid=(1,),
        in_specs=SCALARS + vmem(3) + [pl.BlockSpec(memory_space=pl.ANY)],
        out_specs=tuple(
            vmem(2) + [pl.BlockSpec((groups + 1, 16, LANES), lambda i: (0, last, 0))]
        ),
        input_output_aliases={4: 2},
    )
    near = swap_near(edges, "gx")
    far = swap_far(edges, "gx")
    parity = (lax.axis_index("gx") % 2).astype(jnp.int32).reshape(1)
    lanes = [jnp.repeat(v, WINDOW).reshape(groups, 1, LANES) for v in (diffusivity, reaction_rate)]
    border = call(
        window_kernel,
        jax.ShapeDtypeStruct((SECTIONS, groups, heights, length + 8, LANES), jnp.float32),
        (parity, edges, near, far, *lanes),
        in_specs=SCALARS + vmem(5),
        out_specs=vmem(1)[0],
    )
    return halo_rows, half, border


def sections(first, count, evolved, initial_state, halo_rows, border, half, diffusivity, rate):
    species, heights, length, width = initial_state.shape
    per_group = LANES // WINDOW
    state_spec = pl.BlockSpec((1, heights, length, width), lambda i, f: (f[0] + i, 0, 0, 0))
    in_specs = [
        state_spec,
        pl.BlockSpec((1, 16, width), lambda i, f: (f[0] + i, 0, 0)),
        pl.BlockSpec(
            (SECTIONS, 1, heights, length + 8, LANES),
            lambda i, f: (0, (f[0] + i) // per_group, 0, 0, 0),
        ),
        pl.BlockSpec(half.shape, lambda i, f: (0, 0, 0, 0)),
        pl.BlockSpec(memory_space=pltpu.SMEM),
        pl.BlockSpec(memory_space=pltpu.SMEM),
    ]
    inputs = [first, initial_state, halo_rows, border, half, diffusivity, rate]
    aliases = {}
    if evolved is not None:
        in_specs.append(pl.BlockSpec(memory_space=pl.ANY))
        aliases[len(inputs)] = 0
        inputs.append(evolved)
    return call(
        section_kernel,
        (
            jax.ShapeDtypeStruct(initial_state.shape, jnp.float32),
            jax.ShapeDtypeStruct((count, heights * length, width), jnp.bfloat16),
        ),
        inputs,
        grid_spec=pltpu.PrefetchScalarGridSpec(
            num_scalar_prefetch=1,
            grid=(count,),
            in_specs=in_specs,
            out_specs=(
                state_spec,
                pl.BlockSpec((1, heights * length, width), lambda i, f: (i, 0, 0)),
            ),
        ),
        input_output_aliases=aliases,
    )


def shards(initial_state, velocity, diffusivity, reaction_rate, start_basis):
    species, heights, length, width = initial_state.shape
    pieces = lax.axis_size("gx")
    each = species // pieces
    place = lax.axis_index("gx").astype(jnp.int32)
    halo_rows, half, border = borders(initial_state, velocity, diffusivity, reaction_rate)
    evolved = None
    columns = [None] * pieces
    for offset in reversed(range(pieces)):
        first = ((place ^ offset) * each).reshape(1)
        evolved, piece = sections(
            first,
            each,
            evolved,
            initial_state,
            halo_rows,
            border,
            half,
            diffusivity,
            reaction_rate,
        )
        piece = piece.reshape(each * heights * length, width)
        if offset:
            piece = lax.ppermute(piece, "gx", [(i, i ^ offset) for i in range(pieces)])
        columns[offset] = piece
    own_rows, core = subspace(columns, start_basis)
    return (evolved, own_rows, core.reshape(each, heights, length, start_basis.shape[1]))


def solution(mesh):
    in_specs = (P(None, None, "gy", "gx"), P(None, None, "gy", "gx"), P(), P(), P())
    out_specs = (P(None, None, "gy", "gx"), P(("gx", "gy"), None), P("gx", None, "gy", None))
    return jax.shard_map(shards, mesh=mesh, in_specs=in_specs, out_specs=out_specs, check_vma=False)
```

```python
import functools
import math

import jax
import jax.numpy as jnp
from jax import lax
from jax.experimental import pallas as pl
from jax.experimental.pallas import tpu as pltpu
from jax.sharding import PartitionSpec as P

SECTIONS = 4
NS_STEPS = 5
HIGHEST = lax.Precision.HIGHEST
VMEM_BYTES = 24 * 1024 * 1024
BOTH = ("gx", "gy")
LANES = 128
WIDTH = SECTIONS
WINDOW = 2 * WIDTH


def near_pairs(count):
    return [(i, i ^ 1) for i in range(count)]


def far_pairs(count):
    return [(i, (i + 1) % count if i % 2 else (i - 1) % count) for i in range(count)]


def swap_near(x, axis):
    return lax.ppermute(x, axis, near_pairs(lax.axis_size(axis)))


def swap_far(x, axis):
    return lax.ppermute(x, axis, far_pairs(lax.axis_size(axis)))


def iota(shape, dim):
    return lax.broadcasted_iota(jnp.int32, shape, dim)


def place_edges(tile, slot, packed):
    width = tile.shape[1]
    lane = iota((tile.shape[0], LANES), 1)
    both = tile
    if width > LANES:
        both = jnp.where(lane < WIDTH, tile[:, :LANES], tile[:, width - LANES :])
    rolled = pltpu.roll(both, WIDTH + WINDOW * slot, 1) if WIDTH + WINDOW * slot < LANES else (
        pltpu.roll(both, WIDTH + WINDOW * slot - LANES, 1)
    )
    return jnp.where(lane // WINDOW == slot, rolled, packed)


def pack_kernel(parity_ref, state_ref, velocity_ref, near_ref, far_ref, edges_ref):
    species, heights, length, width = state_ref.shape
    components = velocity_ref.shape[0]
    even = parity_ref[0] == 0
    sub = iota((8, width), 0)

    def edge_rows(ref, at):
        first = [ref[at, z, pl.ds(0, 8), :] for z in range(2)]
        last = [ref[at, z, pl.ds(length - 8, 8), :] for z in range(2)]
        first = jnp.where(sub < WIDTH, first[0], pltpu.roll(first[1], WIDTH, 0))
        last = jnp.where(sub < WIDTH, pltpu.roll(last[0], WIDTH, 0), last[1])
        return jnp.where(even, last, first), jnp.where(even, first, last)

    def put(pair, one, two):
        near_ref[pair] = jnp.concatenate([one[0], two[0]], axis=0).astype(jnp.bfloat16)
        far_ref[pair] = jnp.concatenate([one[1], two[1]], axis=0).astype(jnp.bfloat16)

    def pair_body(pair, carry):
        put(pair, edge_rows(state_ref, 2 * pair), edge_rows(state_ref, 2 * pair + 1))
        return carry

    lax.fori_loop(0, species // 2, pair_body, 0, unroll=2)
    flows = [edge_rows(velocity_ref, at) for at in range(components)]
    put(species // 2, flows[0], flows[1])
    put(species // 2 + 1, flows[2], flows[2])

    per_group = LANES // WINDOW

    def rows_body(at, carry):
        start = pl.multiple_of(at * 16, 16)
        for z in range(heights):
            target = pl.ds(pl.multiple_of(z * length + start, 16), 16)
            for group in range(species // per_group):
                packed = jnp.zeros((16, LANES), jnp.float32)
                for slot in range(per_group):
                    tile = state_ref[group * per_group + slot, z, pl.ds(start, 16), :]
                    packed = place_edges(tile, slot, packed)
                edges_ref[group, target, :] = packed.astype(jnp.bfloat16)
            packed = jnp.zeros((16, LANES), jnp.float32)
            for slot in range(components):
                packed = place_edges(velocity_ref[slot, z, pl.ds(start, 16), :], slot, packed)
            edges_ref[species // per_group, target, :] = packed.astype(jnp.bfloat16)
        return carry

    lax.fori_loop(0, length // 16, rows_body, 0)


def halo_kernel(parity_ref, near_ref, far_ref, velocity_ref, old_ref, rows_ref, half_ref, edges_ref):
    species, _, width = rows_ref.shape
    components, heights, length, _ = velocity_ref.shape
    even = parity_ref[0] == 0
    sub = iota((8, width), 0)
    per_group = LANES // WINDOW

    def tile_of(at):
        near = near_ref[at // 2].astype(jnp.float32)[8 * (at % 2) : 8 * (at % 2) + 8]
        far = far_ref[at // 2].astype(jnp.float32)[8 * (at % 2) : 8 * (at % 2) + 8]
        after = jnp.where(even, near, far)
        before = jnp.where(even, far, near)
        one = jnp.where(sub < WIDTH, after, pltpu.roll(before, WIDTH, 0))
        two = jnp.where(sub < WIDTH, pltpu.roll(after, WIDTH, 0), before)
        return jnp.concatenate([one, two], axis=0)

    for group in range(species // per_group):
        packed = jnp.zeros((16, LANES), jnp.float32)
        for slot in range(per_group):
            tile = tile_of(group * per_group + slot)
            rows_ref[group * per_group + slot] = tile
            packed = place_edges(tile, slot, packed)
        edges_ref[group] = packed.astype(jnp.bfloat16)
    packed = jnp.zeros((16, LANES), jnp.float32)
    for slot in range(components):
        tile = tile_of(species + slot)
        packed = place_edges(tile, slot, packed)
        for z in range(heights):
            factor = -0.5 if slot == 2 and z == 1 else 0.5
            half_ref[slot, z, pl.ds(0, length), :] = factor * velocity_ref[slot, z]
            half_ref[slot, z, pl.ds(length, 8), :] = factor * tile[8 * z : 8 * z + 8]
    edges_ref[species // per_group] = packed.astype(jnp.bfloat16)


def advance(here, other, north, south, east, west, flow, diffusion, rate):
    square = 1.0 + here * here
    inverse = pl.reciprocal(square, approx=True)
    inverse = inverse * (2.0 - square * inverse)
    centre = here * ((1.0 - 6.0 * diffusion - rate) + rate * inverse)
    spread = diffusion * ((east + west) + (north + south))
    moved = flow[0] * (east - west) + flow[1] * (north - south)
    return (centre + other * (diffusion - flow[2])) + (spread - moved)


def window_kernel(parity_ref, own_ref, near_ref, far_ref, spread_ref, rate_ref, border_ref):
    sections, groups, both, _ = border_ref.shape
    heights = 2
    rows = both // heights
    length = rows - 8
    even = parity_ref[0] == 0
    lane = iota((rows, LANES), 1)
    low = lane % WINDOW < WIDTH

    def rows_of(ref, group, z):
        whole = ref[group].astype(jnp.float32)
        body = whole[z * length : (z + 1) * length]
        return jnp.concatenate(
            [body, whole[heights * length + 8 * z : heights * length + 8 * z + 8]], axis=0
        )

    def windows(group):
        out = []
        for z in range(heights):
            own, near, far = [rows_of(r, group, z) for r in (own_ref, near_ref, far_ref)]
            right = jnp.where(even, near, far)
            left = jnp.where(even, far, near)
            out.append((jnp.where(low, left, own), jnp.where(low, own, right)))
        return [[out[z][side] for z in range(heights)] for side in range(2)]

    def spread_lanes(packed, slot):
        part = jnp.where(lane // WINDOW == slot, packed, 0.0)
        step = WINDOW
        while step < LANES:
            part = part + pltpu.roll(part, step, 1)
            step *= 2
        return part

    flows = windows(groups)
    flow = [
        [
            [
                (-0.5 if slot == 2 and z == 1 else 0.5) * spread_lanes(flows[side][z], slot)
                for slot in range(3)
            ]
            for z in range(heights)
        ]
        for side in range(2)
    ]
    for group in range(groups):
        now = windows(group)
        diffusion = spread_ref[group]
        rate = rate_ref[group]
        for section in range(sections):
            border = [jnp.where(low, now[0][z], now[1][z]) for z in range(heights)]
            border_ref[section, group] = jnp.concatenate(border, axis=0).astype(jnp.bfloat16)
            if section == sections - 1:
                break
            now = [
                [
                    advance(
                        now[side][z],
                        now[side][1 - z],
                        pltpu.roll(now[side][z], rows - 1, 0),
                        pltpu.roll(now[side][z], 1, 0),
                        pltpu.roll(now[side][z], LANES - 1, 1),
                        pltpu.roll(now[side][z], 1, 1),
                        flow[side][z],
                        diffusion,
                        rate,
                    )
                    for z in range(heights)
                ]
                for side in range(2)
            ]


def section_kernel(
    pieces, blocks_ref, state_ref, rows_ref, border_ref, half_ref, spread_ref, rate_ref, *rest
):
    evolved_ref, piece_refs = rest[-5 - pieces], rest[-4 - pieces : -4]
    land_ref, work_ref, side_ref, arrived = rest[-4:]
    _, count, heights, length, width = land_ref.shape
    rows = length + 8
    sections = border_ref.shape[0]
    tiles = length // 8
    lane = iota((8, width), 1)
    step = pl.program_id(0)
    now = lax.rem(step, 2)
    first = blocks_ref[step] * count
    diffusion = [spread_ref[first + at] for at in range(count)]
    rate = [rate_ref[first + at] for at in range(count)]

    def fetch(index, into):
        return pltpu.make_async_copy(
            state_ref.at[pl.ds(blocks_ref[index] * count, count)],
            land_ref.at[into],
            arrived.at[into],
        )

    @pl.when(step == 0)
    def _():
        fetch(0, 0).start()

    @pl.when(step + 1 < pieces)
    def _():
        fetch(step + 1, 1 - now).start()

    lane_from, lane_to = iota((LANES, LANES), 0), iota((LANES, LANES), 1)
    for at in range(count):
        base = WINDOW * lax.rem(first + at, LANES // WINDOW) + WIDTH
        west = (lane_from == base - 1) & (lane_to == LANES - 1)
        east = (lane_from == base) & (lane_to == 0)
        chosen = (west | east).astype(jnp.float32).astype(jnp.bfloat16)
        for section in range(sections):
            side_ref[section, at] = jnp.dot(
                border_ref[section, 0], chosen, preferred_element_type=jnp.float32
            )

    fetch(step, now).wait()
    for at in range(count):
        for z in range(heights):
            tile = rows_ref[at, pl.ds(8 * z, 8), :]
            work_ref[0, at, z, pl.ds(8, length), :] = land_ref[now, at, z]
            work_ref[0, at, z, pl.ds(8 + length, 8), :] = tile
            work_ref[0, at, z, pl.ds(0, 8), :] = tile
            work_ref[0, at, z, pl.ds(16 + length, 8), :] = land_ref[now, at, z, pl.ds(0, 8), :]

    for section in range(sections):
        source, target = section % 2, 1 - section % 2
        final = section == sections - 1
        for tile in range(tiles if final else tiles + 1):
            start = 8 * tile
            flow = [
                [half_ref[part, z, pl.ds(start, 8), :] for part in range(3)]
                for z in range(heights)
            ]
            for at in range(count):
                here = [
                    work_ref[source, at, z, pl.ds(8 + start, 8), :] for z in range(heights)
                ]
                for z in range(heights):
                    border = side_ref[section, at, pl.ds(z * rows + start, 8), :]
                    if width > LANES:
                        border = jnp.concatenate([border] * (width // LANES), axis=1)
                    new = advance(
                        here[z],
                        here[1 - z],
                        work_ref[source, at, z, pl.ds(9 + start, 8), :],
                        work_ref[source, at, z, pl.ds(7 + start, 8), :],
                        pltpu.roll(jnp.where(lane == 0, border, here[z]), width - 1, 1),
                        pltpu.roll(jnp.where(lane == width - 1, border, here[z]), 1, 1),
                        flow[z],
                        diffusion[at],
                        rate[at],
                    )
                    if final:
                        evolved_ref[at, z, pl.ds(start, 8), :] = new
                    else:
                        work_ref[target, at, z, pl.ds(8 + start, 8), :] = new
        if not final:
            for at in range(count):
                for z in range(heights):
                    work_ref[target, at, z, pl.ds(0, 8), :] = work_ref[
                        target, at, z, pl.ds(8 + length, 8), :
                    ]
                    work_ref[target, at, z, pl.ds(16 + length, 8), :] = work_ref[
                        target, at, z, pl.ds(8, 8), :
                    ]
    for piece, piece_ref in enumerate(piece_refs):

        @pl.when(step == piece)
        def _(piece_ref=piece_ref):
            for at in range(count):
                for z in range(heights):
                    piece_ref[pl.ds((at * heights + z) * length, length), :] = evolved_ref[
                        at, z
                    ].astype(jnp.bfloat16)


def project_kernel(place_ref, offsets, basis_ref, columns):
    width = columns[0].shape[1]
    project = jnp.zeros((columns[0].shape[0], basis_ref.shape[1]), jnp.float32)
    for offset, column in zip(offsets, columns):
        rows = pl.ds(pl.multiple_of((place_ref[0] ^ offset) * width, width), width)
        project += jnp.dot(column[...], basis_ref[rows, :], preferred_element_type=jnp.float32)
    return project


def early_kernel(offsets, place_ref, basis_ref, *rest):
    rest[-1][...] = project_kernel(place_ref, offsets, basis_ref, rest[:-1])


def image_kernel(late, place_ref, basis_ref, early_ref, *rest):
    columns, image_ref = rest[:-1], rest[-1]
    width = columns[0].shape[1]
    project = early_ref[...] + project_kernel(place_ref, range(late), basis_ref, columns[:late])
    project = project.astype(jnp.bfloat16)
    for piece, column in enumerate(columns):
        rows = pl.ds(pl.multiple_of((place_ref[0] ^ piece) * width, width), width)
        image_ref[rows, :] = lax.dot_general(
            column[...], project, (((0,), (0,)), ((), ())), preferred_element_type=jnp.float32
        ).astype(image_ref.dtype)


def factor_kernel(place_ref, image_ref, *rest):
    columns, (own_ref, core_ref, factor_ref) = rest[:-3], rest[-3:]
    rows, width = columns[0].shape
    rows_all, rank = image_ref.shape
    rows_each = own_ref.shape[0]
    image = image_ref[...]
    identity = (iota((rank, rank), 0) == iota((rank, rank), 1)).astype(jnp.float32)
    gram = lax.dot_general(
        image,
        image,
        (((0,), (0,)), ((), ())),
        precision=HIGHEST,
        preferred_element_type=jnp.float32,
    )
    trace = jnp.sum(gram * identity)
    gram = gram / (trace + 1e-06)
    product = None
    for step in range(NS_STEPS):
        update = 1.5 * identity - 0.5 * gram
        if step < NS_STEPS - 1:
            gram = jnp.dot(gram, update, precision=HIGHEST, preferred_element_type=jnp.float32)
            gram = jnp.dot(update, gram, precision=HIGHEST, preferred_element_type=jnp.float32)
        if product is None:
            product = update
        else:
            product = jnp.dot(
                product, update, precision=HIGHEST, preferred_element_type=jnp.float32
            )
    scaling = jnp.sqrt(rows_all / (trace + 1e-06))
    factor = jnp.dot(
        image * scaling, product, precision=HIGHEST, preferred_element_type=jnp.float32
    )
    factor_ref[...] = factor.astype(jnp.bfloat16)
    start = pl.multiple_of(place_ref[1] * rows_each, rows_each)
    own_ref[...] = factor_ref[pl.ds(start, rows_each), :]
    core = jnp.zeros((rows, rank), jnp.float32)
    for piece, column in enumerate(columns):
        at = pl.ds(pl.multiple_of((place_ref[0] ^ piece) * width, width), width)
        core += jnp.dot(column[...], factor_ref[at, :], preferred_element_type=jnp.float32)
    core_ref[...] = core / math.sqrt(rows_all)


def call(kernel, out_shape, inputs, **rest):
    return pl.pallas_call(
        kernel,
        out_shape=out_shape,
        compiler_params=pltpu.CompilerParams(vmem_limit_bytes=VMEM_BYTES),
        **rest,
    )(*inputs)


def vmem(count):
    return [pl.BlockSpec(memory_space=pltpu.VMEM)] * count


SCALARS = [pl.BlockSpec(memory_space=pltpu.SMEM)]


def subspace(columns, start_basis):
    rows, width = columns[0].shape
    rows_all, rank = start_basis.shape
    owners = lax.axis_size(BOTH)
    rows_each = rows_all // owners
    place = jnp.stack([lax.axis_index("gx"), lax.axis_index(BOTH)]).astype(jnp.int32)
    late = len(columns) // 2
    early = call(
        functools.partial(early_kernel, range(late, len(columns))),
        jax.ShapeDtypeStruct((rows, rank), jnp.float32),
        (place, start_basis, *columns[late:]),
        in_specs=SCALARS + vmem(1 + len(columns) - late),
        out_specs=vmem(1)[0],
    )
    partial = call(
        functools.partial(image_kernel, late),
        jax.ShapeDtypeStruct((rows_all, rank), jnp.bfloat16),
        (place, start_basis, early, *columns),
        in_specs=SCALARS + vmem(2 + len(columns)),
        out_specs=vmem(1)[0],
    )
    shares = lax.all_to_all(
        partial.reshape(owners, rows_each, rank), BOTH, split_axis=0, concat_axis=0, tiled=True
    )
    own_image = jnp.sum(shares.astype(jnp.float32), axis=0)
    image = lax.all_to_all(
        jnp.broadcast_to(own_image[None], (owners, rows_each, rank)),
        BOTH,
        split_axis=0,
        concat_axis=0,
        tiled=True,
    ).reshape(rows_all, rank)
    return call(
        factor_kernel,
        (
            jax.ShapeDtypeStruct((rows_each, rank), jnp.bfloat16),
            jax.ShapeDtypeStruct((rows, rank), jnp.float32),
        ),
        (place, image, *columns),
        in_specs=SCALARS + vmem(1 + len(columns)),
        out_specs=tuple(vmem(2)),
        scratch_shapes=[pltpu.VMEM((rows_all, rank), jnp.bfloat16)],
    )


def borders(initial_state, velocity, diffusivity, reaction_rate):
    species, heights, length, width = initial_state.shape
    groups = species * WINDOW // LANES
    parity = (lax.axis_index("gy") % 2).astype(jnp.int32).reshape(1)
    edge = jax.ShapeDtypeStruct((species // 2 + 2, 16, width), jnp.bfloat16)
    window = jax.ShapeDtypeStruct((groups + 1, heights * (length + 8), LANES), jnp.bfloat16)
    near, far, edges = call(
        pack_kernel,
        (edge, edge, window),
        (parity, initial_state, velocity),
        in_specs=SCALARS + vmem(2),
        out_specs=tuple(vmem(3)),
    )
    near = swap_near(near, "gy")
    far = swap_far(far, "gy")
    last = heights * length // 16
    halo_rows, half, edges = call(
        halo_kernel,
        (
            jax.ShapeDtypeStruct((species, 16, width), jnp.float32),
            jax.ShapeDtypeStruct((3, heights, length + 8, width), jnp.float32),
            window,
        ),
        (parity, near, far, velocity, edges),
        grid=(1,),
        in_specs=SCALARS + vmem(3) + [pl.BlockSpec(memory_space=pl.ANY)],
        out_specs=tuple(
            vmem(2) + [pl.BlockSpec((groups + 1, 16, LANES), lambda i: (0, last, 0))]
        ),
        input_output_aliases={4: 2},
    )
    near = swap_near(edges, "gx")
    far = swap_far(edges, "gx")
    parity = (lax.axis_index("gx") % 2).astype(jnp.int32).reshape(1)
    lanes = [jnp.repeat(v, WINDOW).reshape(groups, 1, LANES) for v in (diffusivity, reaction_rate)]
    border = call(
        window_kernel,
        jax.ShapeDtypeStruct(
            (SECTIONS, groups, heights * (length + 8), LANES), jnp.bfloat16
        ),
        (parity, edges, near, far, *lanes),
        in_specs=SCALARS + vmem(5),
        out_specs=vmem(1)[0],
    )
    return halo_rows, half, border


def sections(blocks, evolved, initial_state, halo_rows, border, half, diffusivity, rate):
    species, heights, length, width = initial_state.shape
    pieces = blocks.shape[0]
    count = species // lax.axis_size("gx")
    per_group = LANES // (WINDOW * count)
    state_spec = pl.BlockSpec((count, heights, length, width), lambda i, f: (f[i], 0, 0, 0))
    in_specs = [
        pl.BlockSpec(memory_space=pltpu.HBM),
        pl.BlockSpec((count, 16, width), lambda i, f: (f[i], 0, 0)),
        pl.BlockSpec(
            (SECTIONS, 1, heights * (length + 8), LANES),
            lambda i, f: (0, f[i] // per_group, 0, 0),
        ),
        pl.BlockSpec(half.shape, lambda i, f: (0, 0, 0, 0)),
        pl.BlockSpec(memory_space=pltpu.SMEM),
        pl.BlockSpec(memory_space=pltpu.SMEM),
    ]
    inputs = [blocks, initial_state, halo_rows, border, half, diffusivity, rate]
    aliases = {}
    if evolved is not None:
        in_specs.append(pl.BlockSpec(memory_space=pl.ANY))
        aliases[len(inputs)] = 0
        inputs.append(evolved)
    rows = count * heights * length
    piece = jax.ShapeDtypeStruct((rows, width), jnp.bfloat16)
    return call(
        functools.partial(section_kernel, pieces),
        (jax.ShapeDtypeStruct(initial_state.shape, jnp.float32),) + (piece,) * pieces,
        inputs,
        grid_spec=pltpu.PrefetchScalarGridSpec(
            num_scalar_prefetch=1,
            grid=(pieces,),
            in_specs=in_specs,
            out_specs=(state_spec,)
            + (pl.BlockSpec((rows, width), lambda i, f: (0, 0)),) * pieces,
            scratch_shapes=[
                pltpu.VMEM((2, count, heights, length, width), jnp.float32),
                pltpu.VMEM((2, count, heights, length + 24, width), jnp.float32),
                pltpu.VMEM((SECTIONS, count, heights * (length + 8), LANES), jnp.float32),
                pltpu.SemaphoreType.DMA((2,)),
            ],
        ),
        input_output_aliases=aliases,
    )


def shards(initial_state, velocity, diffusivity, reaction_rate, start_basis):
    species, heights, length, width = initial_state.shape
    pieces = lax.axis_size("gx")
    each = species // pieces
    place = lax.axis_index("gx").astype(jnp.int32)
    halo_rows, half, border = borders(initial_state, velocity, diffusivity, reaction_rate)
    evolved = None
    columns = [None] * pieces
    for offsets in (range(pieces // 2, pieces), range(pieces // 2)):
        offsets = offsets[::-1]
        evolved, *sent = sections(
            jnp.stack([place ^ offset for offset in offsets]),
            evolved,
            initial_state,
            halo_rows,
            border,
            half,
            diffusivity,
            reaction_rate,
        )
        for offset, piece in zip(offsets, sent):
            if offset:
                piece = lax.ppermute(piece, "gx", [(i, i ^ offset) for i in range(pieces)])
            columns[offset] = piece
    own_rows, core = subspace(columns, start_basis)
    return (evolved, own_rows, core.reshape(each, heights, length, start_basis.shape[1]))


def solution(mesh):
    in_specs = (P(None, None, "gy", "gx"), P(None, None, "gy", "gx"), P(), P(), P())
    out_specs = (P(None, None, "gy", "gx"), P(("gx", "gy"), None), P("gx", None, "gy", None))
    return jax.shard_map(shards, mesh=mesh, in_specs=in_specs, out_specs=out_specs, check_vma=False)
```

```python
import functools
import math

import jax
import jax.numpy as jnp
from jax import lax
from jax.experimental import pallas as pl
from jax.experimental.pallas import tpu as pltpu
from jax.sharding import PartitionSpec as P

SECTIONS = 4
NS_STEPS = 5
HIGHEST = lax.Precision.HIGHEST
VMEM_BYTES = 24 * 1024 * 1024
FULL_VMEM_BYTES = 60 * 1024 * 1024
BOTH = ("gx", "gy")
LANES = 128
WIDTH = SECTIONS
WINDOW = 2 * WIDTH


def near_pairs(count):
    return [(i, i ^ 1) for i in range(count)]


def far_pairs(count):
    return [(i, (i + 1) % count if i % 2 else (i - 1) % count) for i in range(count)]


def swap_near(x, axis):
    return lax.ppermute(x, axis, near_pairs(lax.axis_size(axis)))


def swap_far(x, axis):
    return lax.ppermute(x, axis, far_pairs(lax.axis_size(axis)))


def iota(shape, dim):
    return lax.broadcasted_iota(jnp.int32, shape, dim)


def place_edges(tile, slot, packed):
    width = tile.shape[1]
    lane = iota((tile.shape[0], LANES), 1)
    both = tile
    if width > LANES:
        both = jnp.where(lane < WIDTH, tile[:, :LANES], tile[:, width - LANES :])
    rolled = pltpu.roll(both, WIDTH + WINDOW * slot, 1) if WIDTH + WINDOW * slot < LANES else (
        pltpu.roll(both, WIDTH + WINDOW * slot - LANES, 1)
    )
    return jnp.where(lane // WINDOW == slot, rolled, packed)


def rows_kernel(parity_ref, state_ref, velocity_ref, near_ref, far_ref, first_ref, last_ref, arrived):
    species, _, length, width = state_ref.shape
    components = velocity_ref.shape[0]
    even = parity_ref[0] == 0
    sub = iota((8, width), 0)
    copies = []
    for ref, start, count in ((state_ref, 0, species), (velocity_ref, species, components)):
        for side, land_ref in enumerate((first_ref, last_ref)):
            copies.append(
                pltpu.make_async_copy(
                    ref.at[:, :, pl.ds(side * (length - 8), 8), :],
                    land_ref.at[pl.ds(start, count)],
                    arrived.at[len(copies)],
                )
            )
            copies[-1].start()
    for copy in copies:
        copy.wait()

    def edge_rows(at):
        first = [first_ref[at, z] for z in range(2)]
        last = [last_ref[at, z] for z in range(2)]
        first = jnp.where(sub < WIDTH, first[0], pltpu.roll(first[1], WIDTH, 0))
        last = jnp.where(sub < WIDTH, pltpu.roll(last[0], WIDTH, 0), last[1])
        return jnp.where(even, last, first), jnp.where(even, first, last)

    def put(pair, one, two):
        near_ref[pair] = jnp.concatenate([one[0], two[0]], axis=0).astype(jnp.bfloat16)
        far_ref[pair] = jnp.concatenate([one[1], two[1]], axis=0).astype(jnp.bfloat16)

    for pair in range(species // 2):
        put(pair, edge_rows(2 * pair), edge_rows(2 * pair + 1))
    flows = [edge_rows(species + at) for at in range(components)]
    put(species // 2, flows[0], flows[1])
    put(species // 2 + 1, flows[2], flows[2])


def edges_kernel(state_ref, velocity_ref, edges_ref):
    species, heights, length, _ = state_ref.shape
    components = velocity_ref.shape[0]
    per_group = LANES // WINDOW

    def rows_body(at, carry):
        start = pl.multiple_of(at * 16, 16)
        for z in range(heights):
            target = pl.ds(pl.multiple_of(z * length + start, 16), 16)
            for group in range(species // per_group):
                packed = jnp.zeros((16, LANES), jnp.float32)
                for slot in range(per_group):
                    tile = state_ref[group * per_group + slot, z, pl.ds(start, 16), :]
                    packed = place_edges(tile, slot, packed)
                edges_ref[group, target, :] = packed.astype(jnp.bfloat16)
            packed = jnp.zeros((16, LANES), jnp.float32)
            for slot in range(components):
                packed = place_edges(velocity_ref[slot, z, pl.ds(start, 16), :], slot, packed)
            edges_ref[species // per_group, target, :] = packed.astype(jnp.bfloat16)
        return carry

    lax.fori_loop(0, length // 16, rows_body, 0)


def halo_kernel(parity_ref, near_ref, far_ref, velocity_ref, old_ref, rows_ref, half_ref, edges_ref):
    species, _, width = rows_ref.shape
    components, heights, length, _ = velocity_ref.shape
    even = parity_ref[0] == 0
    sub = iota((8, width), 0)
    per_group = LANES // WINDOW

    def tile_of(at):
        near = near_ref[at // 2].astype(jnp.float32)[8 * (at % 2) : 8 * (at % 2) + 8]
        far = far_ref[at // 2].astype(jnp.float32)[8 * (at % 2) : 8 * (at % 2) + 8]
        after = jnp.where(even, near, far)
        before = jnp.where(even, far, near)
        one = jnp.where(sub < WIDTH, after, pltpu.roll(before, WIDTH, 0))
        two = jnp.where(sub < WIDTH, pltpu.roll(after, WIDTH, 0), before)
        return jnp.concatenate([one, two], axis=0)

    for group in range(species // per_group):
        packed = jnp.zeros((16, LANES), jnp.float32)
        for slot in range(per_group):
            tile = tile_of(group * per_group + slot)
            rows_ref[group * per_group + slot] = tile
            packed = place_edges(tile, slot, packed)
        edges_ref[group] = packed.astype(jnp.bfloat16)
    packed = jnp.zeros((16, LANES), jnp.float32)
    for slot in range(components):
        tile = tile_of(species + slot)
        packed = place_edges(tile, slot, packed)
        for z in range(heights):
            factor = -0.5 if slot == 2 and z == 1 else 0.5
            half_ref[slot, z, pl.ds(0, length), :] = factor * velocity_ref[slot, z]
            half_ref[slot, z, pl.ds(length, 8), :] = factor * tile[8 * z : 8 * z + 8]
    edges_ref[species // per_group] = packed.astype(jnp.bfloat16)


def advance(here, other, north, south, east, west, flow, diffusion, rate):
    square = 1.0 + here * here
    inverse = pl.reciprocal(square, approx=True)
    inverse = inverse * (2.0 - square * inverse)
    centre = here * ((1.0 - 6.0 * diffusion - rate) + rate * inverse)
    spread = diffusion * ((east + west) + (north + south))
    moved = flow[0] * (east - west) + flow[1] * (north - south)
    return (centre + other * (diffusion - flow[2])) + (spread - moved)


def window_kernel(parity_ref, own_ref, near_ref, far_ref, spread_ref, rate_ref, border_ref):
    groups, total, _ = border_ref.shape
    heights, sections = 2, SECTIONS
    both = total // sections
    rows = both // heights
    length = rows - 8
    even = parity_ref[0] == 0
    lane = iota((rows, LANES), 1)
    low = lane % WINDOW < WIDTH

    def rows_of(ref, group, z):
        whole = ref[group].astype(jnp.float32)
        body = whole[z * length : (z + 1) * length]
        return jnp.concatenate(
            [body, whole[heights * length + 8 * z : heights * length + 8 * z + 8]], axis=0
        )

    def windows(group):
        out = []
        for z in range(heights):
            own, near, far = [rows_of(r, group, z) for r in (own_ref, near_ref, far_ref)]
            right = jnp.where(even, near, far)
            left = jnp.where(even, far, near)
            out.append((jnp.where(low, left, own), jnp.where(low, own, right)))
        return [[out[z][side] for z in range(heights)] for side in range(2)]

    def spread_lanes(packed, slot):
        part = jnp.where(lane // WINDOW == slot, packed, 0.0)
        step = WINDOW
        while step < LANES:
            part = part + pltpu.roll(part, step, 1)
            step *= 2
        return part

    flows = windows(groups)
    flow = [
        [
            [
                (-0.5 if slot == 2 and z == 1 else 0.5) * spread_lanes(flows[side][z], slot)
                for slot in range(3)
            ]
            for z in range(heights)
        ]
        for side in range(2)
    ]
    for group in range(groups):
        now = windows(group)
        diffusion = spread_ref[group]
        rate = rate_ref[group]
        for section in range(sections):
            border = [jnp.where(low, now[0][z], now[1][z]) for z in range(heights)]
            border_ref[group, pl.ds(section * both, both), :] = jnp.concatenate(
                border, axis=0
            ).astype(jnp.bfloat16)
            if section == sections - 1:
                break
            now = [
                [
                    advance(
                        now[side][z],
                        now[side][1 - z],
                        pltpu.roll(now[side][z], rows - 1, 0),
                        pltpu.roll(now[side][z], 1, 0),
                        pltpu.roll(now[side][z], LANES - 1, 1),
                        pltpu.roll(now[side][z], 1, 1),
                        flow[side][z],
                        diffusion,
                        rate,
                    )
                    for z in range(heights)
                ]
                for side in range(2)
            ]


def section_kernel(
    pieces, blocks_ref, state_ref, rows_ref, border_ref, half_ref, spread_ref, rate_ref, *rest
):
    evolved_ref, piece_refs = rest[-5 - pieces], rest[-4 - pieces : -4]
    land_ref, work_ref, side_ref, arrived = rest[-4:]
    _, count, heights, length, width = land_ref.shape
    rows = length + 8
    sections = SECTIONS
    tiles = length // 8
    lane = iota((8, width), 1)
    step = pl.program_id(0)
    now = lax.rem(step, 2)
    first = blocks_ref[step] * count
    diffusion = [spread_ref[first + at] for at in range(count)]
    rate = [rate_ref[first + at] for at in range(count)]

    def fetch(index, into):
        return pltpu.make_async_copy(
            state_ref.at[pl.ds(blocks_ref[index] * count, count)],
            land_ref.at[into],
            arrived.at[into],
        )

    @pl.when(step == 0)
    def _():
        fetch(0, 0).start()

    @pl.when(step + 1 < pieces)
    def _():
        fetch(step + 1, 1 - now).start()

    lane_from, lane_to = iota((LANES, LANES), 0), iota((LANES, LANES), 1)
    for at in range(count):
        base = WINDOW * lax.rem(first + at, LANES // WINDOW) + WIDTH
        west = (lane_from == base - 1) & (lane_to == LANES - 1)
        east = (lane_from == base) & (lane_to == 0)
        chosen = (west | east).astype(jnp.float32).astype(jnp.bfloat16)
        side_ref[at] = jnp.dot(border_ref[0], chosen, preferred_element_type=jnp.float32)

    fetch(step, now).wait()
    for at in range(count):
        for z in range(heights):
            tile = rows_ref[at, pl.ds(8 * z, 8), :]
            work_ref[0, at, z, pl.ds(8, length), :] = land_ref[now, at, z]
            work_ref[0, at, z, pl.ds(8 + length, 8), :] = tile
            work_ref[0, at, z, pl.ds(0, 8), :] = tile
            work_ref[0, at, z, pl.ds(16 + length, 8), :] = land_ref[now, at, z, pl.ds(0, 8), :]

    for section in range(sections):
        source, target = section % 2, 1 - section % 2
        final = section == sections - 1
        for tile in range(tiles if final else tiles + 1):
            start = 8 * tile
            flow = [
                [half_ref[part, z, pl.ds(start, 8), :] for part in range(3)]
                for z in range(heights)
            ]
            for at in range(count):
                here = [
                    work_ref[source, at, z, pl.ds(8 + start, 8), :] for z in range(heights)
                ]
                for z in range(heights):
                    border = side_ref[at, pl.ds((section * heights + z) * rows + start, 8), :]
                    if width > LANES:
                        border = jnp.concatenate([border] * (width // LANES), axis=1)
                    new = advance(
                        here[z],
                        here[1 - z],
                        work_ref[source, at, z, pl.ds(9 + start, 8), :],
                        work_ref[source, at, z, pl.ds(7 + start, 8), :],
                        pltpu.roll(jnp.where(lane == 0, border, here[z]), width - 1, 1),
                        pltpu.roll(jnp.where(lane == width - 1, border, here[z]), 1, 1),
                        flow[z],
                        diffusion[at],
                        rate[at],
                    )
                    if final:
                        evolved_ref[at, z, pl.ds(start, 8), :] = new
                    else:
                        work_ref[target, at, z, pl.ds(8 + start, 8), :] = new
        if not final:
            for at in range(count):
                for z in range(heights):
                    work_ref[target, at, z, pl.ds(0, 8), :] = work_ref[
                        target, at, z, pl.ds(8 + length, 8), :
                    ]
                    work_ref[target, at, z, pl.ds(16 + length, 8), :] = work_ref[
                        target, at, z, pl.ds(8, 8), :
                    ]
    for piece, piece_ref in enumerate(piece_refs):

        @pl.when(step == piece)
        def _(piece_ref=piece_ref):
            for at in range(count):
                for z in range(heights):
                    piece_ref[pl.ds((at * heights + z) * length, length), :] = evolved_ref[
                        at, z
                    ].astype(jnp.bfloat16)


def project_kernel(place_ref, offsets, basis_ref, columns):
    width = columns[0].shape[1]
    project = jnp.zeros((columns[0].shape[0], basis_ref.shape[1]), jnp.float32)
    for offset, column in zip(offsets, columns):
        rows = pl.ds(pl.multiple_of((place_ref[0] ^ offset) * width, width), width)
        project += jnp.dot(column[...], basis_ref[rows, :], preferred_element_type=jnp.float32)
    return project


def early_kernel(offsets, place_ref, basis_ref, *rest):
    rest[-1][...] = project_kernel(place_ref, offsets, basis_ref, rest[:-1])


def image_kernel(late, place_ref, basis_ref, early_ref, *rest):
    columns, image_ref = rest[:-1], rest[-1]
    width = columns[0].shape[1]
    project = early_ref[...] + project_kernel(place_ref, range(late), basis_ref, columns[:late])
    project = project.astype(jnp.bfloat16)
    for piece, column in enumerate(columns):
        rows = pl.ds(pl.multiple_of((place_ref[0] ^ piece) * width, width), width)
        image_ref[rows, :] = lax.dot_general(
            column[...], project, (((0,), (0,)), ((), ())), preferred_element_type=jnp.float32
        ).astype(image_ref.dtype)


def factor_kernel(place_ref, image_ref, *rest):
    columns, (own_ref, core_ref, factor_ref) = rest[:-3], rest[-3:]
    rows, width = columns[0].shape
    rows_all, rank = image_ref.shape
    rows_each = own_ref.shape[0]
    image = image_ref[...]
    identity = (iota((rank, rank), 0) == iota((rank, rank), 1)).astype(jnp.float32)
    gram = lax.dot_general(
        image,
        image,
        (((0,), (0,)), ((), ())),
        precision=HIGHEST,
        preferred_element_type=jnp.float32,
    )
    trace = jnp.sum(gram * identity)
    gram = gram / (trace + 1e-06)
    product = None
    for step in range(NS_STEPS):
        update = 1.5 * identity - 0.5 * gram
        if step < NS_STEPS - 1:
            gram = jnp.dot(gram, update, precision=HIGHEST, preferred_element_type=jnp.float32)
            gram = jnp.dot(update, gram, precision=HIGHEST, preferred_element_type=jnp.float32)
        if product is None:
            product = update
        else:
            product = jnp.dot(
                product, update, precision=HIGHEST, preferred_element_type=jnp.float32
            )
    scaling = jnp.sqrt(rows_all / (trace + 1e-06))
    factor = jnp.dot(
        image * scaling, product, precision=HIGHEST, preferred_element_type=jnp.float32
    )
    factor_ref[...] = factor.astype(jnp.bfloat16)
    start = pl.multiple_of(place_ref[1] * rows_each, rows_each)
    own_ref[...] = factor_ref[pl.ds(start, rows_each), :]
    core = jnp.zeros((rows, rank), jnp.float32)
    for piece, column in enumerate(columns):
        at = pl.ds(pl.multiple_of((place_ref[0] ^ piece) * width, width), width)
        core += jnp.dot(column[...], factor_ref[at, :], preferred_element_type=jnp.float32)
    core_ref[...] = core / math.sqrt(rows_all)


def call(kernel, out_shape, inputs, vmem_bytes=VMEM_BYTES, **rest):
    return pl.pallas_call(
        kernel,
        out_shape=out_shape,
        compiler_params=pltpu.CompilerParams(vmem_limit_bytes=vmem_bytes),
        **rest,
    )(*inputs)


def vmem(count):
    return [pl.BlockSpec(memory_space=pltpu.VMEM)] * count


SCALARS = [pl.BlockSpec(memory_space=pltpu.SMEM)]


def subspace(columns, start_basis):
    rows, width = columns[0].shape
    rows_all, rank = start_basis.shape
    owners = lax.axis_size(BOTH)
    rows_each = rows_all // owners
    place = jnp.stack([lax.axis_index("gx"), lax.axis_index(BOTH)]).astype(jnp.int32)
    late = len(columns) // 2
    early = call(
        functools.partial(early_kernel, range(late, len(columns))),
        jax.ShapeDtypeStruct((rows, rank), jnp.float32),
        (place, start_basis, *columns[late:]),
        in_specs=SCALARS + vmem(1 + len(columns) - late),
        out_specs=vmem(1)[0],
    )
    partial = call(
        functools.partial(image_kernel, late),
        jax.ShapeDtypeStruct((rows_all, rank), jnp.bfloat16),
        (place, start_basis, early, *columns),
        in_specs=SCALARS + vmem(2 + len(columns)),
        out_specs=vmem(1)[0],
    )
    shares = lax.all_to_all(
        partial.reshape(owners, rows_each, rank), BOTH, split_axis=0, concat_axis=0, tiled=True
    )
    own_image = jnp.sum(shares.astype(jnp.float32), axis=0)
    image = lax.all_to_all(
        jnp.broadcast_to(own_image[None], (owners, rows_each, rank)),
        BOTH,
        split_axis=0,
        concat_axis=0,
        tiled=True,
    ).reshape(rows_all, rank)
    return call(
        factor_kernel,
        (
            jax.ShapeDtypeStruct((rows_each, rank), jnp.bfloat16),
            jax.ShapeDtypeStruct((rows, rank), jnp.float32),
        ),
        (place, image, *columns),
        in_specs=SCALARS + vmem(1 + len(columns)),
        out_specs=tuple(vmem(2)),
        scratch_shapes=[pltpu.VMEM((rows_all, rank), jnp.bfloat16)],
    )


def borders(initial_state, velocity, diffusivity, reaction_rate):
    species, heights, length, width = initial_state.shape
    groups = species * WINDOW // LANES
    parity = (lax.axis_index("gy") % 2).astype(jnp.int32).reshape(1)
    edge = jax.ShapeDtypeStruct((species // 2 + 2, 16, width), jnp.bfloat16)
    window = jax.ShapeDtypeStruct((groups + 1, heights * (length + 8), LANES), jnp.bfloat16)
    fields = species + velocity.shape[0]
    land = pltpu.VMEM((fields, heights, 8, width), jnp.float32)
    near, far = call(
        rows_kernel,
        (edge, edge),
        (parity, initial_state, velocity),
        in_specs=SCALARS + [pl.BlockSpec(memory_space=pltpu.HBM)] * 2,
        out_specs=tuple(vmem(2)),
        scratch_shapes=[land, land, pltpu.SemaphoreType.DMA((4,))],
        vmem_bytes=FULL_VMEM_BYTES,
    )
    edges = call(
        edges_kernel,
        window,
        (initial_state, velocity),
        in_specs=vmem(2),
        out_specs=vmem(1)[0],
    )
    near = swap_near(near, "gy")
    far = swap_far(far, "gy")
    last = heights * length // 16
    halo_rows, half, edges = call(
        halo_kernel,
        (
            jax.ShapeDtypeStruct((species, 16, width), jnp.float32),
            jax.ShapeDtypeStruct((3, heights, length + 8, width), jnp.float32),
            window,
        ),
        (parity, near, far, velocity, edges),
        grid=(1,),
        in_specs=SCALARS + vmem(3) + [pl.BlockSpec(memory_space=pl.ANY)],
        out_specs=tuple(
            vmem(2) + [pl.BlockSpec((groups + 1, 16, LANES), lambda i: (0, last, 0))]
        ),
        input_output_aliases={4: 2},
    )
    near = swap_near(edges, "gx")
    far = swap_far(edges, "gx")
    parity = (lax.axis_index("gx") % 2).astype(jnp.int32).reshape(1)
    lanes = [jnp.repeat(v, WINDOW).reshape(groups, 1, LANES) for v in (diffusivity, reaction_rate)]
    border = call(
        window_kernel,
        jax.ShapeDtypeStruct(
            (groups, SECTIONS * heights * (length + 8), LANES), jnp.bfloat16
        ),
        (parity, edges, near, far, *lanes),
        in_specs=SCALARS + vmem(5),
        out_specs=vmem(1)[0],
    )
    return halo_rows, half, border


def sections(blocks, evolved, initial_state, halo_rows, border, half, diffusivity, rate):
    species, heights, length, width = initial_state.shape
    pieces = blocks.shape[0]
    count = species // lax.axis_size("gx")
    per_group = LANES // (WINDOW * count)
    state_spec = pl.BlockSpec((count, heights, length, width), lambda i, f: (f[i], 0, 0, 0))
    in_specs = [
        pl.BlockSpec(memory_space=pltpu.HBM),
        pl.BlockSpec((count, 16, width), lambda i, f: (f[i], 0, 0)),
        pl.BlockSpec(
            (1, SECTIONS * heights * (length + 8), LANES),
            lambda i, f: (f[i] // per_group, 0, 0),
        ),
        pl.BlockSpec(half.shape, lambda i, f: (0, 0, 0, 0)),
        pl.BlockSpec(memory_space=pltpu.SMEM),
        pl.BlockSpec(memory_space=pltpu.SMEM),
    ]
    inputs = [blocks, initial_state, halo_rows, border, half, diffusivity, rate]
    aliases = {}
    if evolved is not None:
        in_specs.append(pl.BlockSpec(memory_space=pl.ANY))
        aliases[len(inputs)] = 0
        inputs.append(evolved)
    rows = count * heights * length
    piece = jax.ShapeDtypeStruct((rows, width), jnp.bfloat16)
    return call(
        functools.partial(section_kernel, pieces),
        (jax.ShapeDtypeStruct(initial_state.shape, jnp.float32),) + (piece,) * pieces,
        inputs,
        grid_spec=pltpu.PrefetchScalarGridSpec(
            num_scalar_prefetch=1,
            grid=(pieces,),
            in_specs=in_specs,
            out_specs=(state_spec,)
            + (pl.BlockSpec((rows, width), lambda i, f: (0, 0)),) * pieces,
            scratch_shapes=[
                pltpu.VMEM((2, count, heights, length, width), jnp.float32),
                pltpu.VMEM((2, count, heights, length + 24, width), jnp.float32),
                pltpu.VMEM((count, SECTIONS * heights * (length + 8), LANES), jnp.float32),
                pltpu.SemaphoreType.DMA((2,)),
            ],
        ),
        input_output_aliases=aliases,
    )


def shards(initial_state, velocity, diffusivity, reaction_rate, start_basis):
    species, heights, length, width = initial_state.shape
    pieces = lax.axis_size("gx")
    each = species // pieces
    place = lax.axis_index("gx").astype(jnp.int32)
    halo_rows, half, border = borders(initial_state, velocity, diffusivity, reaction_rate)
    evolved = None
    columns = [None] * pieces
    half_way, quarter = pieces // 2, pieces // 4
    for offsets in (
        [*range(half_way, half_way + quarter)],
        [*range(half_way + quarter, pieces), *range(1, half_way)],
        [0],
    ):
        evolved, *sent = sections(
            jnp.stack([place ^ offset for offset in offsets]),
            evolved,
            initial_state,
            halo_rows,
            border,
            half,
            diffusivity,
            reaction_rate,
        )
        for offset, piece in zip(offsets, sent):
            if offset:
                piece = lax.ppermute(piece, "gx", [(i, i ^ offset) for i in range(pieces)])
            columns[offset] = piece
    own_rows, core = subspace(columns, start_basis)
    return (evolved, own_rows, core.reshape(each, heights, length, start_basis.shape[1]))


def solution(mesh):
    in_specs = (P(None, None, "gy", "gx"), P(None, None, "gy", "gx"), P(), P(), P())
    out_specs = (P(None, None, "gy", "gx"), P(("gx", "gy"), None), P("gx", None, "gy", None))
    return jax.shard_map(shards, mesh=mesh, in_specs=in_specs, out_specs=out_specs, check_vma=False)
```

```python
import functools
import math

import jax
import jax.numpy as jnp
from jax import lax
from jax.experimental import pallas as pl
from jax.experimental.pallas import tpu as pltpu
from jax.sharding import PartitionSpec as P

SECTIONS = 4
NS_STEPS = 5
HIGHEST = lax.Precision.HIGHEST
VMEM_BYTES = 24 * 1024 * 1024
FULL_VMEM_BYTES = 60 * 1024 * 1024
BOTH = ("gx", "gy")
LANES = 128
WIDTH = SECTIONS
WINDOW = 2 * WIDTH


def near_pairs(count):
    return [(i, i ^ 1) for i in range(count)]


def far_pairs(count):
    return [(i, (i + 1) % count if i % 2 else (i - 1) % count) for i in range(count)]


def swap_near(x, axis):
    return lax.ppermute(x, axis, near_pairs(lax.axis_size(axis)))


def swap_far(x, axis):
    return lax.ppermute(x, axis, far_pairs(lax.axis_size(axis)))


def iota(shape, dim):
    return lax.broadcasted_iota(jnp.int32, shape, dim)


def place_edges(tile, slot, packed):
    width = tile.shape[1]
    lane = iota((tile.shape[0], LANES), 1)
    both = tile
    if width > LANES:
        both = jnp.where(lane < WIDTH, tile[:, :LANES], tile[:, width - LANES :])
    rolled = pltpu.roll(both, WIDTH + WINDOW * slot, 1) if WIDTH + WINDOW * slot < LANES else (
        pltpu.roll(both, WIDTH + WINDOW * slot - LANES, 1)
    )
    return jnp.where(lane // WINDOW == slot, rolled, packed)


def rows_kernel(parity_ref, state_ref, velocity_ref, near_ref, far_ref, first_ref, last_ref, arrived):
    species, _, length, width = state_ref.shape
    components = velocity_ref.shape[0]
    even = parity_ref[0] == 0
    sub = iota((8, width), 0)
    copies = []
    for ref, start, count in ((state_ref, 0, species), (velocity_ref, species, components)):
        for side, land_ref in enumerate((first_ref, last_ref)):
            copies.append(
                pltpu.make_async_copy(
                    ref.at[:, :, pl.ds(side * (length - 8), 8), :],
                    land_ref.at[pl.ds(start, count)],
                    arrived.at[len(copies)],
                )
            )
            copies[-1].start()
    for copy in copies:
        copy.wait()

    def edge_rows(at):
        first = [first_ref[at, z] for z in range(2)]
        last = [last_ref[at, z] for z in range(2)]
        first = jnp.where(sub < WIDTH, first[0], pltpu.roll(first[1], WIDTH, 0))
        last = jnp.where(sub < WIDTH, pltpu.roll(last[0], WIDTH, 0), last[1])
        return jnp.where(even, last, first), jnp.where(even, first, last)

    def put(pair, one, two):
        near_ref[pair] = jnp.concatenate([one[0], two[0]], axis=0).astype(jnp.bfloat16)
        far_ref[pair] = jnp.concatenate([one[1], two[1]], axis=0).astype(jnp.bfloat16)

    for pair in range(species // 2):
        put(pair, edge_rows(2 * pair), edge_rows(2 * pair + 1))
    flows = [edge_rows(species + at) for at in range(components)]
    put(species // 2, flows[0], flows[1])
    put(species // 2 + 1, flows[2], flows[2])


def edges_kernel(state_ref, velocity_ref, edges_ref):
    species, heights, length, _ = state_ref.shape
    components = velocity_ref.shape[0]
    per_group = LANES // WINDOW

    def rows_body(at, carry):
        start = pl.multiple_of(at * 16, 16)
        for z in range(heights):
            target = pl.ds(pl.multiple_of(z * length + start, 16), 16)
            for group in range(species // per_group):
                packed = jnp.zeros((16, LANES), jnp.float32)
                for slot in range(per_group):
                    tile = state_ref[group * per_group + slot, z, pl.ds(start, 16), :]
                    packed = place_edges(tile, slot, packed)
                edges_ref[group, target, :] = packed.astype(jnp.bfloat16)
            packed = jnp.zeros((16, LANES), jnp.float32)
            for slot in range(components):
                packed = place_edges(velocity_ref[slot, z, pl.ds(start, 16), :], slot, packed)
            edges_ref[species // per_group, target, :] = packed.astype(jnp.bfloat16)
        return carry

    lax.fori_loop(0, length // 16, rows_body, 0)


def halo_kernel(parity_ref, near_ref, far_ref, velocity_ref, old_ref, rows_ref, half_ref, edges_ref):
    species, _, width = rows_ref.shape
    components, heights, length, _ = velocity_ref.shape
    even = parity_ref[0] == 0
    sub = iota((8, width), 0)
    per_group = LANES // WINDOW

    def tile_of(at):
        near = near_ref[at // 2].astype(jnp.float32)[8 * (at % 2) : 8 * (at % 2) + 8]
        far = far_ref[at // 2].astype(jnp.float32)[8 * (at % 2) : 8 * (at % 2) + 8]
        after = jnp.where(even, near, far)
        before = jnp.where(even, far, near)
        one = jnp.where(sub < WIDTH, after, pltpu.roll(before, WIDTH, 0))
        two = jnp.where(sub < WIDTH, pltpu.roll(after, WIDTH, 0), before)
        return jnp.concatenate([one, two], axis=0)

    for group in range(species // per_group):
        packed = jnp.zeros((16, LANES), jnp.float32)
        for slot in range(per_group):
            tile = tile_of(group * per_group + slot)
            rows_ref[group * per_group + slot] = tile
            packed = place_edges(tile, slot, packed)
        edges_ref[group] = packed.astype(jnp.bfloat16)
    packed = jnp.zeros((16, LANES), jnp.float32)
    for slot in range(components):
        tile = tile_of(species + slot)
        packed = place_edges(tile, slot, packed)
        for z in range(heights):
            factor = -0.5 if slot == 2 and z == 1 else 0.5
            half_ref[slot, z, pl.ds(0, length), :] = factor * velocity_ref[slot, z]
            half_ref[slot, z, pl.ds(length, 8), :] = factor * tile[8 * z : 8 * z + 8]
    edges_ref[species // per_group] = packed.astype(jnp.bfloat16)


def advance(here, other, north, south, east, west, flow, diffusion, rate):
    square = 1.0 + here * here
    inverse = pl.reciprocal(square, approx=True)
    inverse = inverse * (2.0 - square * inverse)
    centre = here * ((1.0 - 6.0 * diffusion - rate) + rate * inverse)
    spread = diffusion * ((east + west) + (north + south))
    moved = flow[0] * (east - west) + flow[1] * (north - south)
    return (centre + other * (diffusion - flow[2])) + (spread - moved)


def window_kernel(parity_ref, own_ref, near_ref, far_ref, spread_ref, rate_ref, border_ref):
    groups, total, _ = border_ref.shape
    heights, sections = 2, SECTIONS
    both = total // sections
    rows = both // heights
    length = rows - 8
    even = parity_ref[0] == 0
    lane = iota((rows, LANES), 1)
    low = lane % WINDOW < WIDTH

    def rows_of(ref, group, z):
        whole = ref[group].astype(jnp.float32)
        body = whole[z * length : (z + 1) * length]
        return jnp.concatenate(
            [body, whole[heights * length + 8 * z : heights * length + 8 * z + 8]], axis=0
        )

    def windows(group):
        out = []
        for z in range(heights):
            own, near, far = [rows_of(r, group, z) for r in (own_ref, near_ref, far_ref)]
            right = jnp.where(even, near, far)
            left = jnp.where(even, far, near)
            out.append((jnp.where(low, left, own), jnp.where(low, own, right)))
        return [[out[z][side] for z in range(heights)] for side in range(2)]

    flows = windows(groups)
    packed = jnp.concatenate([flow for side in flows for flow in side], axis=0)
    packed = packed.astype(jnp.bfloat16)
    lane_from, lane_to = iota((LANES, LANES), 0), iota((LANES, LANES), 1)

    def spread_lanes(slot):
        chosen = (lane_from // WINDOW == slot) & (lane_from % WINDOW == lane_to % WINDOW)
        chosen = chosen.astype(jnp.float32).astype(jnp.bfloat16)
        return jnp.dot(packed, chosen, preferred_element_type=jnp.float32)

    spread = [spread_lanes(slot) for slot in range(3)]
    flow = [
        [
            [
                (-0.5 if slot == 2 and z == 1 else 0.5)
                * spread[slot][(side * heights + z) * rows : (side * heights + z + 1) * rows]
                for slot in range(3)
            ]
            for z in range(heights)
        ]
        for side in range(2)
    ]
    for group in range(groups):
        now = windows(group)
        diffusion = spread_ref[group]
        rate = rate_ref[group]
        for section in range(sections):
            border = [jnp.where(low, now[0][z], now[1][z]) for z in range(heights)]
            border_ref[group, pl.ds(section * both, both), :] = jnp.concatenate(
                border, axis=0
            ).astype(jnp.bfloat16)
            if section == sections - 1:
                break
            now = [
                [
                    advance(
                        now[side][z],
                        now[side][1 - z],
                        pltpu.roll(now[side][z], rows - 1, 0),
                        pltpu.roll(now[side][z], 1, 0),
                        pltpu.roll(now[side][z], LANES - 1, 1),
                        pltpu.roll(now[side][z], 1, 1),
                        flow[side][z],
                        diffusion,
                        rate,
                    )
                    for z in range(heights)
                ]
                for side in range(2)
            ]


def section_kernel(
    pieces, blocks_ref, state_ref, rows_ref, border_ref, half_ref, spread_ref, rate_ref, *rest
):
    evolved_ref, piece_refs = rest[-5 - pieces], rest[-4 - pieces : -4]
    land_ref, work_ref, side_ref, arrived = rest[-4:]
    _, count, heights, length, width = land_ref.shape
    rows = length + 8
    sections = SECTIONS
    tiles = length // 8
    lane = iota((8, width), 1)
    step = pl.program_id(0)
    now = lax.rem(step, 2)
    first = blocks_ref[step] * count
    diffusion = [spread_ref[first + at] for at in range(count)]
    rate = [rate_ref[first + at] for at in range(count)]

    def fetch(index, into):
        return pltpu.make_async_copy(
            state_ref.at[pl.ds(blocks_ref[index] * count, count)],
            land_ref.at[into],
            arrived.at[into],
        )

    @pl.when(step == 0)
    def _():
        fetch(0, 0).start()

    @pl.when(step + 1 < pieces)
    def _():
        fetch(step + 1, 1 - now).start()

    lane_from, lane_to = iota((LANES, LANES), 0), iota((LANES, LANES), 1)
    for at in range(count):
        base = WINDOW * lax.rem(first + at, LANES // WINDOW) + WIDTH
        west = (lane_from == base - 1) & (lane_to == LANES - 1)
        east = (lane_from == base) & (lane_to == 0)
        chosen = (west | east).astype(jnp.float32).astype(jnp.bfloat16)
        side_ref[at] = jnp.dot(border_ref[0], chosen, preferred_element_type=jnp.float32)

    fetch(step, now).wait()
    for at in range(count):
        for z in range(heights):
            tile = rows_ref[at, pl.ds(8 * z, 8), :]
            work_ref[0, at, z, pl.ds(8, length), :] = land_ref[now, at, z]
            work_ref[0, at, z, pl.ds(8 + length, 8), :] = tile
            work_ref[0, at, z, pl.ds(0, 8), :] = tile
            work_ref[0, at, z, pl.ds(16 + length, 8), :] = land_ref[now, at, z, pl.ds(0, 8), :]

    for section in range(sections):
        source, target = section % 2, 1 - section % 2
        final = section == sections - 1
        for tile in range(tiles if final else tiles + 1):
            start = 8 * tile
            flow = [
                [half_ref[part, z, pl.ds(start, 8), :] for part in range(3)]
                for z in range(heights)
            ]
            for at in range(count):
                here = [
                    work_ref[source, at, z, pl.ds(8 + start, 8), :] for z in range(heights)
                ]
                for z in range(heights):
                    border = side_ref[at, pl.ds((section * heights + z) * rows + start, 8), :]
                    if width > LANES:
                        border = jnp.concatenate([border] * (width // LANES), axis=1)
                    new = advance(
                        here[z],
                        here[1 - z],
                        work_ref[source, at, z, pl.ds(9 + start, 8), :],
                        work_ref[source, at, z, pl.ds(7 + start, 8), :],
                        pltpu.roll(jnp.where(lane == 0, border, here[z]), width - 1, 1),
                        pltpu.roll(jnp.where(lane == width - 1, border, here[z]), 1, 1),
                        flow[z],
                        diffusion[at],
                        rate[at],
                    )
                    if final:
                        evolved_ref[at, z, pl.ds(start, 8), :] = new
                    else:
                        work_ref[target, at, z, pl.ds(8 + start, 8), :] = new
        if not final:
            for at in range(count):
                for z in range(heights):
                    work_ref[target, at, z, pl.ds(0, 8), :] = work_ref[
                        target, at, z, pl.ds(8 + length, 8), :
                    ]
                    work_ref[target, at, z, pl.ds(16 + length, 8), :] = work_ref[
                        target, at, z, pl.ds(8, 8), :
                    ]
    for piece, piece_ref in enumerate(piece_refs):

        @pl.when(step == piece)
        def _(piece_ref=piece_ref):
            for at in range(count):
                for z in range(heights):
                    piece_ref[pl.ds((at * heights + z) * length, length), :] = evolved_ref[
                        at, z
                    ].astype(jnp.bfloat16)


def project_kernel(place_ref, offsets, basis_ref, columns):
    width = columns[0].shape[1]
    project = jnp.zeros((columns[0].shape[0], basis_ref.shape[1]), jnp.float32)
    for offset, column in zip(offsets, columns):
        rows = pl.ds(pl.multiple_of((place_ref[0] ^ offset) * width, width), width)
        project += jnp.dot(column[...], basis_ref[rows, :], preferred_element_type=jnp.float32)
    return project


def early_kernel(offsets, place_ref, basis_ref, *rest):
    rest[-1][...] = project_kernel(place_ref, offsets, basis_ref, rest[:-1])


def image_kernel(late, place_ref, basis_ref, early_ref, *rest):
    columns, image_ref = rest[:-1], rest[-1]
    width = columns[0].shape[1]
    project = early_ref[...] + project_kernel(place_ref, range(late), basis_ref, columns[:late])
    project = project.astype(jnp.bfloat16)
    for piece, column in enumerate(columns):
        rows = pl.ds(pl.multiple_of((place_ref[0] ^ piece) * width, width), width)
        image_ref[rows, :] = lax.dot_general(
            column[...], project, (((0,), (0,)), ((), ())), preferred_element_type=jnp.float32
        ).astype(image_ref.dtype)


def factor_kernel(place_ref, image_ref, *rest):
    columns, (own_ref, core_ref, factor_ref) = rest[:-3], rest[-3:]
    rows, width = columns[0].shape
    rows_all, rank = image_ref.shape
    rows_each = own_ref.shape[0]
    image = image_ref[...]
    identity = (iota((rank, rank), 0) == iota((rank, rank), 1)).astype(jnp.float32)
    gram = lax.dot_general(
        image,
        image,
        (((0,), (0,)), ((), ())),
        precision=HIGHEST,
        preferred_element_type=jnp.float32,
    )
    trace = jnp.sum(gram * identity)
    gram = gram / (trace + 1e-06)
    product = None
    for step in range(NS_STEPS):
        update = 1.5 * identity - 0.5 * gram
        if step < NS_STEPS - 1:
            gram = jnp.dot(gram, update, precision=HIGHEST, preferred_element_type=jnp.float32)
            gram = jnp.dot(update, gram, precision=HIGHEST, preferred_element_type=jnp.float32)
        if product is None:
            product = update
        else:
            product = jnp.dot(
                product, update, precision=HIGHEST, preferred_element_type=jnp.float32
            )
    scaling = jnp.sqrt(rows_all / (trace + 1e-06))
    factor = jnp.dot(
        image * scaling, product, precision=HIGHEST, preferred_element_type=jnp.float32
    )
    factor_ref[...] = factor.astype(jnp.bfloat16)
    start = pl.multiple_of(place_ref[1] * rows_each, rows_each)
    own_ref[...] = factor_ref[pl.ds(start, rows_each), :]
    core = jnp.zeros((rows, rank), jnp.float32)
    for piece, column in enumerate(columns):
        at = pl.ds(pl.multiple_of((place_ref[0] ^ piece) * width, width), width)
        core += jnp.dot(column[...], factor_ref[at, :], preferred_element_type=jnp.float32)
    core_ref[...] = core / math.sqrt(rows_all)


def call(kernel, out_shape, inputs, vmem_bytes=VMEM_BYTES, **rest):
    return pl.pallas_call(
        kernel,
        out_shape=out_shape,
        compiler_params=pltpu.CompilerParams(vmem_limit_bytes=vmem_bytes),
        **rest,
    )(*inputs)


def vmem(count):
    return [pl.BlockSpec(memory_space=pltpu.VMEM)] * count


SCALARS = [pl.BlockSpec(memory_space=pltpu.SMEM)]


def subspace(columns, start_basis):
    rows, width = columns[0].shape
    rows_all, rank = start_basis.shape
    owners = lax.axis_size(BOTH)
    rows_each = rows_all // owners
    place = jnp.stack([lax.axis_index("gx"), lax.axis_index(BOTH)]).astype(jnp.int32)
    late = len(columns) // 2
    early = call(
        functools.partial(early_kernel, range(late, len(columns))),
        jax.ShapeDtypeStruct((rows, rank), jnp.float32),
        (place, start_basis, *columns[late:]),
        in_specs=SCALARS + vmem(1 + len(columns) - late),
        out_specs=vmem(1)[0],
    )
    partial = call(
        functools.partial(image_kernel, late),
        jax.ShapeDtypeStruct((rows_all, rank), jnp.bfloat16),
        (place, start_basis, early, *columns),
        in_specs=SCALARS + vmem(2 + len(columns)),
        out_specs=vmem(1)[0],
    )
    shares = lax.all_to_all(
        partial.reshape(owners, rows_each, rank), BOTH, split_axis=0, concat_axis=0, tiled=True
    )
    own_image = jnp.sum(shares.astype(jnp.float32), axis=0)
    image = lax.all_to_all(
        jnp.broadcast_to(own_image[None], (owners, rows_each, rank)),
        BOTH,
        split_axis=0,
        concat_axis=0,
        tiled=True,
    ).reshape(rows_all, rank)
    return call(
        factor_kernel,
        (
            jax.ShapeDtypeStruct((rows_each, rank), jnp.bfloat16),
            jax.ShapeDtypeStruct((rows, rank), jnp.float32),
        ),
        (place, image, *columns),
        in_specs=SCALARS + vmem(1 + len(columns)),
        out_specs=tuple(vmem(2)),
        scratch_shapes=[pltpu.VMEM((rows_all, rank), jnp.bfloat16)],
    )


def borders(initial_state, velocity, diffusivity, reaction_rate):
    species, heights, length, width = initial_state.shape
    groups = species * WINDOW // LANES
    parity = (lax.axis_index("gy") % 2).astype(jnp.int32).reshape(1)
    edge = jax.ShapeDtypeStruct((species // 2 + 2, 16, width), jnp.bfloat16)
    window = jax.ShapeDtypeStruct((groups + 1, heights * (length + 8), LANES), jnp.bfloat16)
    fields = species + velocity.shape[0]
    land = pltpu.VMEM((fields, heights, 8, width), jnp.float32)
    near, far = call(
        rows_kernel,
        (edge, edge),
        (parity, initial_state, velocity),
        in_specs=SCALARS + [pl.BlockSpec(memory_space=pltpu.HBM)] * 2,
        out_specs=tuple(vmem(2)),
        scratch_shapes=[land, land, pltpu.SemaphoreType.DMA((4,))],
        vmem_bytes=FULL_VMEM_BYTES,
    )
    edges = call(
        edges_kernel,
        window,
        (initial_state, velocity),
        in_specs=vmem(2),
        out_specs=vmem(1)[0],
    )
    near = swap_near(near, "gy")
    far = swap_far(far, "gy")
    last = heights * length // 16
    halo_rows, half, edges = call(
        halo_kernel,
        (
            jax.ShapeDtypeStruct((species, 16, width), jnp.float32),
            jax.ShapeDtypeStruct((3, heights, length + 8, width), jnp.float32),
            window,
        ),
        (parity, near, far, velocity, edges),
        grid=(1,),
        in_specs=SCALARS + vmem(3) + [pl.BlockSpec(memory_space=pl.ANY)],
        out_specs=tuple(
            vmem(2) + [pl.BlockSpec((groups + 1, 16, LANES), lambda i: (0, last, 0))]
        ),
        input_output_aliases={4: 2},
    )
    near = swap_near(edges, "gx")
    far = swap_far(edges, "gx")
    parity = (lax.axis_index("gx") % 2).astype(jnp.int32).reshape(1)
    lanes = [jnp.repeat(v, WINDOW).reshape(groups, 1, LANES) for v in (diffusivity, reaction_rate)]
    border = call(
        window_kernel,
        jax.ShapeDtypeStruct(
            (groups, SECTIONS * heights * (length + 8), LANES), jnp.bfloat16
        ),
        (parity, edges, near, far, *lanes),
        in_specs=SCALARS + vmem(5),
        out_specs=vmem(1)[0],
    )
    return halo_rows, half, border


def sections(blocks, evolved, initial_state, halo_rows, border, half, diffusivity, rate):
    species, heights, length, width = initial_state.shape
    pieces = blocks.shape[0]
    count = species // lax.axis_size("gx")
    per_group = LANES // (WINDOW * count)
    state_spec = pl.BlockSpec((count, heights, length, width), lambda i, f: (f[i], 0, 0, 0))
    in_specs = [
        pl.BlockSpec(memory_space=pltpu.HBM),
        pl.BlockSpec((count, 16, width), lambda i, f: (f[i], 0, 0)),
        pl.BlockSpec(
            (1, SECTIONS * heights * (length + 8), LANES),
            lambda i, f: (f[i] // per_group, 0, 0),
        ),
        pl.BlockSpec(half.shape, lambda i, f: (0, 0, 0, 0)),
        pl.BlockSpec(memory_space=pltpu.SMEM),
        pl.BlockSpec(memory_space=pltpu.SMEM),
    ]
    inputs = [blocks, initial_state, halo_rows, border, half, diffusivity, rate]
    aliases = {}
    if evolved is not None:
        in_specs.append(pl.BlockSpec(memory_space=pl.ANY))
        aliases[len(inputs)] = 0
        inputs.append(evolved)
    rows = count * heights * length
    piece = jax.ShapeDtypeStruct((rows, width), jnp.bfloat16)
    return call(
        functools.partial(section_kernel, pieces),
        (jax.ShapeDtypeStruct(initial_state.shape, jnp.float32),) + (piece,) * pieces,
        inputs,
        grid_spec=pltpu.PrefetchScalarGridSpec(
            num_scalar_prefetch=1,
            grid=(pieces,),
            in_specs=in_specs,
            out_specs=(state_spec,)
            + (pl.BlockSpec((rows, width), lambda i, f: (0, 0)),) * pieces,
            scratch_shapes=[
                pltpu.VMEM((2, count, heights, length, width), jnp.float32),
                pltpu.VMEM((2, count, heights, length + 24, width), jnp.float32),
                pltpu.VMEM((count, SECTIONS * heights * (length + 8), LANES), jnp.float32),
                pltpu.SemaphoreType.DMA((2,)),
            ],
        ),
        input_output_aliases=aliases,
    )


def shards(initial_state, velocity, diffusivity, reaction_rate, start_basis):
    species, heights, length, width = initial_state.shape
    pieces = lax.axis_size("gx")
    each = species // pieces
    place = lax.axis_index("gx").astype(jnp.int32)
    halo_rows, half, border = borders(initial_state, velocity, diffusivity, reaction_rate)
    evolved = None
    columns = [None] * pieces
    half_way, quarter = pieces // 2, pieces // 4
    for offsets in (
        [*range(half_way, half_way + quarter)],
        [*range(half_way + quarter, pieces), *range(1, half_way)],
        [0],
    ):
        evolved, *sent = sections(
            jnp.stack([place ^ offset for offset in offsets]),
            evolved,
            initial_state,
            halo_rows,
            border,
            half,
            diffusivity,
            reaction_rate,
        )
        for offset, piece in zip(offsets, sent):
            if offset:
                piece = lax.ppermute(piece, "gx", [(i, i ^ offset) for i in range(pieces)])
            columns[offset] = piece
    own_rows, core = subspace(columns, start_basis)
    return (evolved, own_rows, core.reshape(each, heights, length, start_basis.shape[1]))


def solution(mesh):
    in_specs = (P(None, None, "gy", "gx"), P(None, None, "gy", "gx"), P(), P(), P())
    out_specs = (P(None, None, "gy", "gx"), P(("gx", "gy"), None), P("gx", None, "gy", None))
    return jax.shard_map(shards, mesh=mesh, in_specs=in_specs, out_specs=out_specs, check_vma=False)
```

```python
import functools
import math

import jax
import jax.numpy as jnp
from jax import lax
from jax.experimental import pallas as pl
from jax.experimental.pallas import tpu as pltpu
from jax.sharding import PartitionSpec as P

SECTIONS = 4
NS_STEPS = 5
HIGHEST = lax.Precision.HIGHEST
VMEM_BYTES = 24 * 1024 * 1024
FULL_VMEM_BYTES = 60 * 1024 * 1024
BOTH = ("gx", "gy")
LANES = 128
WIDTH = SECTIONS
WINDOW = 2 * WIDTH


def near_pairs(count):
    return [(i, i ^ 1) for i in range(count)]


def far_pairs(count):
    return [(i, (i + 1) % count if i % 2 else (i - 1) % count) for i in range(count)]


def swap_near(x, axis):
    return lax.ppermute(x, axis, near_pairs(lax.axis_size(axis)))


def swap_far(x, axis):
    return lax.ppermute(x, axis, far_pairs(lax.axis_size(axis)))


def iota(shape, dim):
    return lax.broadcasted_iota(jnp.int32, shape, dim)


def place_edges(tile, slot, packed):
    width = tile.shape[1]
    lane = iota((tile.shape[0], LANES), 1)
    both = tile
    if width > LANES:
        both = jnp.where(lane < WIDTH, tile[:, :LANES], tile[:, width - LANES :])
    rolled = pltpu.roll(both, WIDTH + WINDOW * slot, 1) if WIDTH + WINDOW * slot < LANES else (
        pltpu.roll(both, WIDTH + WINDOW * slot - LANES, 1)
    )
    return jnp.where(lane // WINDOW == slot, rolled, packed)


def rows_kernel(parity_ref, state_ref, velocity_ref, near_ref, far_ref, first_ref, last_ref, arrived):
    species, _, length, width = state_ref.shape
    components = velocity_ref.shape[0]
    even = parity_ref[0] == 0
    sub = iota((8, width), 0)
    copies = []
    for ref, start, count in ((state_ref, 0, species), (velocity_ref, species, components)):
        for side, land_ref in enumerate((first_ref, last_ref)):
            copies.append(
                pltpu.make_async_copy(
                    ref.at[:, :, pl.ds(side * (length - 8), 8), :],
                    land_ref.at[pl.ds(start, count)],
                    arrived.at[len(copies)],
                )
            )
            copies[-1].start()
    for copy in copies:
        copy.wait()

    def edge_rows(at):
        first = [first_ref[at, z] for z in range(2)]
        last = [last_ref[at, z] for z in range(2)]
        first = jnp.where(sub < WIDTH, first[0], pltpu.roll(first[1], WIDTH, 0))
        last = jnp.where(sub < WIDTH, pltpu.roll(last[0], WIDTH, 0), last[1])
        return jnp.where(even, last, first), jnp.where(even, first, last)

    def put(pair, one, two):
        near_ref[pair] = jnp.concatenate([one[0], two[0]], axis=0).astype(jnp.bfloat16)
        far_ref[pair] = jnp.concatenate([one[1], two[1]], axis=0).astype(jnp.bfloat16)

    for pair in range(species // 2):
        put(pair, edge_rows(2 * pair), edge_rows(2 * pair + 1))
    flows = [edge_rows(species + at) for at in range(components)]
    put(species // 2, flows[0], flows[1])
    put(species // 2 + 1, flows[2], flows[2])


def edges_kernel(state_ref, velocity_ref, edges_ref):
    species, heights, length, _ = state_ref.shape
    components = velocity_ref.shape[0]
    per_group = LANES // WINDOW

    def rows_body(at, carry):
        start = pl.multiple_of(at * 16, 16)
        for z in range(heights):
            target = pl.ds(pl.multiple_of(z * length + start, 16), 16)
            for group in range(species // per_group):
                packed = jnp.zeros((16, LANES), jnp.float32)
                for slot in range(per_group):
                    tile = state_ref[group * per_group + slot, z, pl.ds(start, 16), :]
                    packed = place_edges(tile, slot, packed)
                edges_ref[group, target, :] = packed.astype(jnp.bfloat16)
            packed = jnp.zeros((16, LANES), jnp.float32)
            for slot in range(components):
                packed = place_edges(velocity_ref[slot, z, pl.ds(start, 16), :], slot, packed)
            edges_ref[species // per_group, target, :] = packed.astype(jnp.bfloat16)
        return carry

    lax.fori_loop(0, length // 16, rows_body, 0)


def halo_kernel(parity_ref, near_ref, far_ref, velocity_ref, old_ref, rows_ref, half_ref, edges_ref):
    species, _, width = rows_ref.shape
    components, heights, length, _ = velocity_ref.shape
    even = parity_ref[0] == 0
    sub = iota((8, width), 0)
    per_group = LANES // WINDOW

    def tile_of(at):
        near = near_ref[at // 2].astype(jnp.float32)[8 * (at % 2) : 8 * (at % 2) + 8]
        far = far_ref[at // 2].astype(jnp.float32)[8 * (at % 2) : 8 * (at % 2) + 8]
        after = jnp.where(even, near, far)
        before = jnp.where(even, far, near)
        one = jnp.where(sub < WIDTH, after, pltpu.roll(before, WIDTH, 0))
        two = jnp.where(sub < WIDTH, pltpu.roll(after, WIDTH, 0), before)
        return jnp.concatenate([one, two], axis=0)

    for group in range(species // per_group):
        packed = jnp.zeros((16, LANES), jnp.float32)
        for slot in range(per_group):
            tile = tile_of(group * per_group + slot)
            rows_ref[group * per_group + slot] = tile
            packed = place_edges(tile, slot, packed)
        edges_ref[group] = packed.astype(jnp.bfloat16)
    packed = jnp.zeros((16, LANES), jnp.float32)
    for slot in range(components):
        tile = tile_of(species + slot)
        packed = place_edges(tile, slot, packed)
        for z in range(heights):
            factor = -0.5 if slot == 2 and z == 1 else 0.5
            half_ref[slot, z, pl.ds(0, length), :] = factor * velocity_ref[slot, z]
            half_ref[slot, z, pl.ds(length, 8), :] = factor * tile[8 * z : 8 * z + 8]
    edges_ref[species // per_group] = packed.astype(jnp.bfloat16)


def advance(here, other, north, south, east, west, flow, diffusion, rate):
    square = 1.0 + here * here
    inverse = pl.reciprocal(square, approx=True)
    inverse = inverse * (2.0 - square * inverse)
    centre = here * ((1.0 - 6.0 * diffusion - rate) + rate * inverse)
    spread = diffusion * ((east + west) + (north + south))
    moved = flow[0] * (east - west) + flow[1] * (north - south)
    return (centre + other * (diffusion - flow[2])) + (spread - moved)


def window_kernel(parity_ref, own_ref, near_ref, far_ref, spread_ref, rate_ref, border_ref):
    groups, total, _ = border_ref.shape
    heights, sections = 2, SECTIONS
    both = total // sections
    rows = both // heights
    length = rows - 8
    even = parity_ref[0] == 0
    lane = iota((rows, LANES), 1)
    low = lane % WINDOW < WIDTH

    def rows_of(ref, group, z):
        whole = ref[group].astype(jnp.float32)
        body = whole[z * length : (z + 1) * length]
        return jnp.concatenate(
            [body, whole[heights * length + 8 * z : heights * length + 8 * z + 8]], axis=0
        )

    def windows(group):
        out = []
        for z in range(heights):
            own, near, far = [rows_of(r, group, z) for r in (own_ref, near_ref, far_ref)]
            right = jnp.where(even, near, far)
            left = jnp.where(even, far, near)
            out.append((jnp.where(low, left, own), jnp.where(low, own, right)))
        return [[out[z][side] for z in range(heights)] for side in range(2)]

    flows = windows(groups)
    packed = jnp.concatenate([flow for side in flows for flow in side], axis=0)
    packed = packed.astype(jnp.bfloat16)
    lane_from, lane_to = iota((LANES, LANES), 0), iota((LANES, LANES), 1)

    def spread_lanes(slot):
        chosen = (lane_from // WINDOW == slot) & (lane_from % WINDOW == lane_to % WINDOW)
        chosen = chosen.astype(jnp.float32).astype(jnp.bfloat16)
        return jnp.dot(packed, chosen, preferred_element_type=jnp.float32)

    spread = [spread_lanes(slot) for slot in range(3)]
    flow = [
        [
            [
                (-0.5 if slot == 2 and z == 1 else 0.5)
                * spread[slot][(side * heights + z) * rows : (side * heights + z + 1) * rows]
                for slot in range(3)
            ]
            for z in range(heights)
        ]
        for side in range(2)
    ]
    for group in range(groups):
        now = windows(group)
        diffusion = spread_ref[group]
        rate = rate_ref[group]
        for section in range(sections):
            border = [jnp.where(low, now[0][z], now[1][z]) for z in range(heights)]
            border_ref[group, pl.ds(section * both, both), :] = jnp.concatenate(
                border, axis=0
            ).astype(jnp.bfloat16)
            if section == sections - 1:
                break
            now = [
                [
                    advance(
                        now[side][z],
                        now[side][1 - z],
                        pltpu.roll(now[side][z], rows - 1, 0),
                        pltpu.roll(now[side][z], 1, 0),
                        pltpu.roll(now[side][z], LANES - 1, 1),
                        pltpu.roll(now[side][z], 1, 1),
                        flow[side][z],
                        diffusion,
                        rate,
                    )
                    for z in range(heights)
                ]
                for side in range(2)
            ]


def section_kernel(
    pieces, blocks_ref, state_ref, rows_ref, border_ref, half_ref, spread_ref, rate_ref, *rest
):
    evolved_ref, piece_refs = rest[-5 - pieces], rest[-4 - pieces : -4]
    land_ref, work_ref, side_ref, arrived = rest[-4:]
    _, count, heights, length, width = land_ref.shape
    rows = length + 8
    sections = SECTIONS
    tiles = length // 8
    lane = iota((8, width), 1)
    step = pl.program_id(0)
    now = lax.rem(step, 2)
    first = blocks_ref[step] * count
    diffusion = [spread_ref[first + at] for at in range(count)]
    rate = [rate_ref[first + at] for at in range(count)]

    def fetch(index, into):
        return pltpu.make_async_copy(
            state_ref.at[pl.ds(blocks_ref[index] * count, count)],
            land_ref.at[into],
            arrived.at[into],
        )

    @pl.when(step == 0)
    def _():
        fetch(0, 0).start()

    @pl.when(step + 1 < pieces)
    def _():
        fetch(step + 1, 1 - now).start()

    lane_from, lane_to = iota((LANES, LANES), 0), iota((LANES, LANES), 1)
    def chosen(at):
        base = WINDOW * lax.rem(first + at, LANES // WINDOW) + WIDTH
        west = (lane_from == base - 1) & (lane_to == LANES - 1)
        east = (lane_from == base) & (lane_to == 0)
        return (west | east).astype(jnp.float32).astype(jnp.bfloat16)

    for at in range(0, count, 2):
        pair = jnp.concatenate([chosen(at), chosen(at + 1)], axis=1)
        aligned = jnp.dot(border_ref[0], pair, preferred_element_type=jnp.float32)
        side_ref[at] = aligned[:, :LANES]
        side_ref[at + 1] = aligned[:, LANES:]

    fetch(step, now).wait()
    for at in range(count):
        for z in range(heights):
            tile = rows_ref[at, pl.ds(8 * z, 8), :]
            work_ref[0, at, z, pl.ds(8, length), :] = land_ref[now, at, z]
            work_ref[0, at, z, pl.ds(8 + length, 8), :] = tile
            work_ref[0, at, z, pl.ds(0, 8), :] = tile
            work_ref[0, at, z, pl.ds(16 + length, 8), :] = land_ref[now, at, z, pl.ds(0, 8), :]

    for section in range(sections):
        source, target = section % 2, 1 - section % 2
        final = section == sections - 1
        for tile in range(tiles if final else tiles + 1):
            start = 8 * tile
            flow = [
                [half_ref[part, z, pl.ds(start, 8), :] for part in range(3)]
                for z in range(heights)
            ]
            for at in range(count):
                here = [
                    work_ref[source, at, z, pl.ds(8 + start, 8), :] for z in range(heights)
                ]
                for z in range(heights):
                    border = side_ref[at, pl.ds((section * heights + z) * rows + start, 8), :]
                    if width > LANES:
                        border = jnp.concatenate([border] * (width // LANES), axis=1)
                    new = advance(
                        here[z],
                        here[1 - z],
                        work_ref[source, at, z, pl.ds(9 + start, 8), :],
                        work_ref[source, at, z, pl.ds(7 + start, 8), :],
                        pltpu.roll(jnp.where(lane == 0, border, here[z]), width - 1, 1),
                        pltpu.roll(jnp.where(lane == width - 1, border, here[z]), 1, 1),
                        flow[z],
                        diffusion[at],
                        rate[at],
                    )
                    if final:
                        evolved_ref[at, z, pl.ds(start, 8), :] = new
                    else:
                        work_ref[target, at, z, pl.ds(8 + start, 8), :] = new
        if not final:
            for at in range(count):
                for z in range(heights):
                    work_ref[target, at, z, pl.ds(0, 8), :] = work_ref[
                        target, at, z, pl.ds(8 + length, 8), :
                    ]
                    work_ref[target, at, z, pl.ds(16 + length, 8), :] = work_ref[
                        target, at, z, pl.ds(8, 8), :
                    ]
    for piece, piece_ref in enumerate(piece_refs):

        @pl.when(step == piece)
        def _(piece_ref=piece_ref):
            for at in range(count):
                for z in range(heights):
                    piece_ref[pl.ds((at * heights + z) * length, length), :] = evolved_ref[
                        at, z
                    ].astype(jnp.bfloat16)


def project_kernel(place_ref, offsets, basis_ref, columns):
    width = columns[0].shape[1]
    project = jnp.zeros((columns[0].shape[0], basis_ref.shape[1]), jnp.float32)
    for offset, column in zip(offsets, columns):
        rows = pl.ds(pl.multiple_of((place_ref[0] ^ offset) * width, width), width)
        project += jnp.dot(column[...], basis_ref[rows, :], preferred_element_type=jnp.float32)
    return project


def early_kernel(offsets, place_ref, basis_ref, *rest):
    rest[-1][...] = project_kernel(place_ref, offsets, basis_ref, rest[:-1])


def image_kernel(late, place_ref, basis_ref, early_ref, *rest):
    columns, image_ref = rest[:-1], rest[-1]
    width = columns[0].shape[1]
    project = early_ref[...] + project_kernel(place_ref, range(late), basis_ref, columns[:late])
    project = project.astype(jnp.bfloat16)
    for piece, column in enumerate(columns):
        rows = pl.ds(pl.multiple_of((place_ref[0] ^ piece) * width, width), width)
        image_ref[rows, :] = lax.dot_general(
            column[...], project, (((0,), (0,)), ((), ())), preferred_element_type=jnp.float32
        ).astype(image_ref.dtype)


def factor_kernel(place_ref, image_ref, *rest):
    columns, (own_ref, core_ref, factor_ref) = rest[:-3], rest[-3:]
    rows, width = columns[0].shape
    rows_all, rank = image_ref.shape
    rows_each = own_ref.shape[0]
    image = image_ref[...]
    identity = (iota((rank, rank), 0) == iota((rank, rank), 1)).astype(jnp.float32)
    gram = lax.dot_general(
        image,
        image,
        (((0,), (0,)), ((), ())),
        precision=HIGHEST,
        preferred_element_type=jnp.float32,
    )
    trace = jnp.sum(gram * identity)
    gram = gram / (trace + 1e-06)
    product = None
    for step in range(NS_STEPS):
        update = 1.5 * identity - 0.5 * gram
        if step < NS_STEPS - 1:
            gram = jnp.dot(gram, update, precision=HIGHEST, preferred_element_type=jnp.float32)
            gram = jnp.dot(update, gram, precision=HIGHEST, preferred_element_type=jnp.float32)
        if product is None:
            product = update
        else:
            product = jnp.dot(
                product, update, precision=HIGHEST, preferred_element_type=jnp.float32
            )
    scaling = jnp.sqrt(rows_all / (trace + 1e-06))
    factor = jnp.dot(
        image * scaling, product, precision=HIGHEST, preferred_element_type=jnp.float32
    )
    factor_ref[...] = factor.astype(jnp.bfloat16)
    start = pl.multiple_of(place_ref[1] * rows_each, rows_each)
    own_ref[...] = factor_ref[pl.ds(start, rows_each), :]
    core = jnp.zeros((rows, rank), jnp.float32)
    for piece, column in enumerate(columns):
        at = pl.ds(pl.multiple_of((place_ref[0] ^ piece) * width, width), width)
        core += jnp.dot(column[...], factor_ref[at, :], preferred_element_type=jnp.float32)
    core_ref[...] = core / math.sqrt(rows_all)


def call(kernel, out_shape, inputs, vmem_bytes=VMEM_BYTES, **rest):
    return pl.pallas_call(
        kernel,
        out_shape=out_shape,
        compiler_params=pltpu.CompilerParams(vmem_limit_bytes=vmem_bytes),
        **rest,
    )(*inputs)


def vmem(count):
    return [pl.BlockSpec(memory_space=pltpu.VMEM)] * count


SCALARS = [pl.BlockSpec(memory_space=pltpu.SMEM)]


def subspace(columns, start_basis):
    rows, width = columns[0].shape
    rows_all, rank = start_basis.shape
    owners = lax.axis_size(BOTH)
    rows_each = rows_all // owners
    place = jnp.stack([lax.axis_index("gx"), lax.axis_index(BOTH)]).astype(jnp.int32)
    late = len(columns) // 2
    early = call(
        functools.partial(early_kernel, range(late, len(columns))),
        jax.ShapeDtypeStruct((rows, rank), jnp.float32),
        (place, start_basis, *columns[late:]),
        in_specs=SCALARS + vmem(1 + len(columns) - late),
        out_specs=vmem(1)[0],
    )
    partial = call(
        functools.partial(image_kernel, late),
        jax.ShapeDtypeStruct((rows_all, rank), jnp.bfloat16),
        (place, start_basis, early, *columns),
        in_specs=SCALARS + vmem(2 + len(columns)),
        out_specs=vmem(1)[0],
    )
    shares = lax.all_to_all(
        partial.reshape(owners, rows_each, rank), BOTH, split_axis=0, concat_axis=0, tiled=True
    )
    own_image = jnp.sum(shares.astype(jnp.float32), axis=0)
    image = lax.all_to_all(
        jnp.broadcast_to(own_image[None], (owners, rows_each, rank)),
        BOTH,
        split_axis=0,
        concat_axis=0,
        tiled=True,
    ).reshape(rows_all, rank)
    return call(
        factor_kernel,
        (
            jax.ShapeDtypeStruct((rows_each, rank), jnp.bfloat16),
            jax.ShapeDtypeStruct((rows, rank), jnp.float32),
        ),
        (place, image, *columns),
        in_specs=SCALARS + vmem(1 + len(columns)),
        out_specs=tuple(vmem(2)),
        scratch_shapes=[pltpu.VMEM((rows_all, rank), jnp.bfloat16)],
    )


def borders(initial_state, velocity, diffusivity, reaction_rate):
    species, heights, length, width = initial_state.shape
    groups = species * WINDOW // LANES
    parity = (lax.axis_index("gy") % 2).astype(jnp.int32).reshape(1)
    edge = jax.ShapeDtypeStruct((species // 2 + 2, 16, width), jnp.bfloat16)
    window = jax.ShapeDtypeStruct((groups + 1, heights * (length + 8), LANES), jnp.bfloat16)
    fields = species + velocity.shape[0]
    land = pltpu.VMEM((fields, heights, 8, width), jnp.float32)
    near, far = call(
        rows_kernel,
        (edge, edge),
        (parity, initial_state, velocity),
        in_specs=SCALARS + [pl.BlockSpec(memory_space=pltpu.HBM)] * 2,
        out_specs=tuple(vmem(2)),
        scratch_shapes=[land, land, pltpu.SemaphoreType.DMA((4,))],
        vmem_bytes=FULL_VMEM_BYTES,
    )
    edges = call(
        edges_kernel,
        window,
        (initial_state, velocity),
        in_specs=vmem(2),
        out_specs=vmem(1)[0],
    )
    near = swap_near(near, "gy")
    far = swap_far(far, "gy")
    last = heights * length // 16
    halo_rows, half, edges = call(
        halo_kernel,
        (
            jax.ShapeDtypeStruct((species, 16, width), jnp.float32),
            jax.ShapeDtypeStruct((3, heights, length + 8, width), jnp.float32),
            window,
        ),
        (parity, near, far, velocity, edges),
        grid=(1,),
        in_specs=SCALARS + vmem(3) + [pl.BlockSpec(memory_space=pl.ANY)],
        out_specs=tuple(
            vmem(2) + [pl.BlockSpec((groups + 1, 16, LANES), lambda i: (0, last, 0))]
        ),
        input_output_aliases={4: 2},
    )
    near = swap_near(edges, "gx")
    far = swap_far(edges, "gx")
    parity = (lax.axis_index("gx") % 2).astype(jnp.int32).reshape(1)
    lanes = [jnp.repeat(v, WINDOW).reshape(groups, 1, LANES) for v in (diffusivity, reaction_rate)]
    border = call(
        window_kernel,
        jax.ShapeDtypeStruct(
            (groups, SECTIONS * heights * (length + 8), LANES), jnp.bfloat16
        ),
        (parity, edges, near, far, *lanes),
        in_specs=SCALARS + vmem(5),
        out_specs=vmem(1)[0],
    )
    return halo_rows, half, border


def sections(blocks, evolved, initial_state, halo_rows, border, half, diffusivity, rate):
    species, heights, length, width = initial_state.shape
    pieces = blocks.shape[0]
    count = species // lax.axis_size("gx")
    per_group = LANES // (WINDOW * count)
    state_spec = pl.BlockSpec((count, heights, length, width), lambda i, f: (f[i], 0, 0, 0))
    in_specs = [
        pl.BlockSpec(memory_space=pltpu.HBM),
        pl.BlockSpec((count, 16, width), lambda i, f: (f[i], 0, 0)),
        pl.BlockSpec(
            (1, SECTIONS * heights * (length + 8), LANES),
            lambda i, f: (f[i] // per_group, 0, 0),
        ),
        pl.BlockSpec(half.shape, lambda i, f: (0, 0, 0, 0)),
        pl.BlockSpec(memory_space=pltpu.SMEM),
        pl.BlockSpec(memory_space=pltpu.SMEM),
    ]
    inputs = [blocks, initial_state, halo_rows, border, half, diffusivity, rate]
    aliases = {}
    if evolved is not None:
        in_specs.append(pl.BlockSpec(memory_space=pl.ANY))
        aliases[len(inputs)] = 0
        inputs.append(evolved)
    rows = count * heights * length
    piece = jax.ShapeDtypeStruct((rows, width), jnp.bfloat16)
    return call(
        functools.partial(section_kernel, pieces),
        (jax.ShapeDtypeStruct(initial_state.shape, jnp.float32),) + (piece,) * pieces,
        inputs,
        grid_spec=pltpu.PrefetchScalarGridSpec(
            num_scalar_prefetch=1,
            grid=(pieces,),
            in_specs=in_specs,
            out_specs=(state_spec,)
            + (pl.BlockSpec((rows, width), lambda i, f: (0, 0)),) * pieces,
            scratch_shapes=[
                pltpu.VMEM((2, count, heights, length, width), jnp.float32),
                pltpu.VMEM((2, count, heights, length + 24, width), jnp.float32),
                pltpu.VMEM((count, SECTIONS * heights * (length + 8), LANES), jnp.float32),
                pltpu.SemaphoreType.DMA((2,)),
            ],
        ),
        input_output_aliases=aliases,
    )


def shards(initial_state, velocity, diffusivity, reaction_rate, start_basis):
    species, heights, length, width = initial_state.shape
    pieces = lax.axis_size("gx")
    each = species // pieces
    place = lax.axis_index("gx").astype(jnp.int32)
    halo_rows, half, border = borders(initial_state, velocity, diffusivity, reaction_rate)
    evolved = None
    columns = [None] * pieces
    half_way, quarter = pieces // 2, pieces // 4
    for offsets in (
        [*range(half_way, half_way + quarter)],
        [*range(half_way + quarter, pieces), *range(1, half_way)],
        [0],
    ):
        evolved, *sent = sections(
            jnp.stack([place ^ offset for offset in offsets]),
            evolved,
            initial_state,
            halo_rows,
            border,
            half,
            diffusivity,
            reaction_rate,
        )
        for offset, piece in zip(offsets, sent):
            if offset:
                piece = lax.ppermute(piece, "gx", [(i, i ^ offset) for i in range(pieces)])
            columns[offset] = piece
    own_rows, core = subspace(columns, start_basis)
    return (evolved, own_rows, core.reshape(each, heights, length, start_basis.shape[1]))


def solution(mesh):
    in_specs = (P(None, None, "gy", "gx"), P(None, None, "gy", "gx"), P(), P(), P())
    out_specs = (P(None, None, "gy", "gx"), P(("gx", "gy"), None), P("gx", None, "gy", None))
    return jax.shard_map(shards, mesh=mesh, in_specs=in_specs, out_specs=out_specs, check_vma=False)
```
